512 devices in a mesh: dom: 64 (over x, z), col: 8 (over y, core).
Axes of the slice: x: 4, y: 4, z: 16, core: 2. Of those that a mesh axis runs over, the one named last changes fastest.
Arguments:
- tiles: bfloat16 [6144, 128, 128], P('dom'), may hold values from -0.21875 to 0.21875
- tile_rows: int32 [6144], P('dom'), may hold values from 0 to 15, as said below
- tile_srcs: int32 [6144], P('dom'), may hold values from 0 to 79, as said below
- send_rows: int32 [64, 64], P('dom'), may hold values from 0 to 15
- basis: bfloat16 [256, 131072], P('col', 'dom')
- rotation: bfloat16 [256, 256], P(None, 'col'), may hold values from -0.375 to 0.375
Outputs:
- gram: float32 [256, 256], P(None, 'col')
- rotated: bfloat16 [256, 131072], P('col', 'dom')
The draws below stay inside these ranges and needn't reach their ends.
Inputs may be any that keep to these rules, and one draw needn't show every extreme that they name: `tile_rows`: every one of a device's 16 row blocks holds one or more of its tiles. `tile_srcs`: a device's pool is its own 16 row blocks followed by the block received from each of the 64 devices of dom in order; each received block is named by exactly one tile of the device.
All inputs are finite; a program needn't handle non-finite values.
Results may differ from the reference program's by a relative error of at most 0.0052.
The reference program's roundings to bfloat16 on the way count: a program that leaves them out, or rounds other values in their place, can miss the bound.
Values may be sent and summed in bfloat16 or wider, within the bound.
A program may use at most 64 MiB of HBM per device.

```python
import math
import jax
import jax.numpy as jnp
from jax import lax

TILE = 128
K = 256
RB = 16
TPD = 96
NROWS = 131072
N_DOM = 64


def draw_tile_rows(key, part):
    key = jax.random.fold_in(key, 7)

    def one(sub):
        cover = jax.random.permutation(jax.random.fold_in(sub, 1), RB).astype(jnp.int32)
        extra = jax.random.randint(jax.random.fold_in(sub, 2), (TPD,), 0, RB).astype(jnp.int32)
        places = jnp.arange(TPD, dtype=jnp.int32)
        values = jnp.where(places < RB, cover[jnp.minimum(places, RB - 1)], extra)
        order = jax.random.permutation(jax.random.fold_in(sub, 3), TPD)
        return values[order]
    keys = jax.random.split(key, N_DOM)
    return jax.vmap(one)(keys).reshape(N_DOM * TPD).astype(jnp.int32)


def draw_tile_srcs(key, part):
    key = jax.random.fold_in(key, 11)

    def one(sub):
        inner = jax.random.randint(jax.random.fold_in(sub, 1), (TPD,), 0, RB).astype(jnp.int32)
        places = jnp.arange(TPD, dtype=jnp.int32)
        values = jnp.where(places < N_DOM, RB + places, inner)
        order = jax.random.permutation(jax.random.fold_in(sub, 2), TPD)
        return values[order]
    keys = jax.random.split(key, N_DOM)
    return jax.vmap(one)(keys).reshape(N_DOM * TPD).astype(jnp.int32)


def draw_send_rows(key, part):
    key = jax.random.fold_in(key, 17)
    flat = jax.random.randint(jax.random.fold_in(key, 1), (N_DOM * N_DOM,), 0, RB).astype(jnp.int32)
    spots = jax.random.permutation(jax.random.fold_in(key, 2), N_DOM * N_DOM)[:RB]
    flat = flat.at[spots].set(jnp.arange(RB, dtype=jnp.int32))
    return flat.reshape(N_DOM, N_DOM)


def draw_basis(key, part):
    key = jax.random.fold_in(key, 29)
    first_key, row_key, col_key = jax.random.split(key, 3)
    place = jnp.arange(NROWS, dtype=jnp.float32) / NROWS
    row_rough = jnp.exp(jax.random.uniform(row_key, (NROWS,), jnp.float32, math.log(0.5), math.log(1.5)))
    row_scale = jnp.exp(math.log(3.0) * place) * row_rough
    col_scale = jnp.exp(jax.random.uniform(col_key, (K, 1), jnp.float32, math.log(0.3), math.log(3.0)))
    base = jax.random.normal(first_key, (K, NROWS), jnp.float32)
    return (0.4 * base * col_scale * row_scale[None, :]).astype(jnp.bfloat16)


def block_scale(stream_key, extent, shards, least, high):
    def one(axis_at, shards_of):
        steps = jax.random.uniform(jax.random.fold_in(jax.random.fold_in(stream_key, 6), axis_at), (shards_of,), jnp.float32, least / len(shards), high / len(shards))
        return jnp.repeat(jnp.exp(steps), extent[axis_at] // shards_of).reshape((-1,) + (1,) * (len(extent) - axis_at - 1))

    gain = one(*shards[0])
    for cut in shards[1:]:
        gain = gain * one(*cut)
    return gain


def bell_draw(stream_key, dims, scale, bound, shards=(), kind=jnp.bfloat16):
    loudness = block_scale(stream_key, dims, shards, -0.22, 0.18) if shards else 1.0
    array = jax.random.normal(stream_key, dims, jnp.float32) * scale * loudness
    return jnp.minimum(jnp.maximum(array, -bound), bound).astype(kind)


def setup_inputs(seed: int = 0) -> dict:
    streams_of = jax.random.split(jax.random.key(seed), 7)
    tiles = bell_draw(streams_of[0], (N_DOM * TPD, TILE, TILE), (TILE * TPD // RB) ** -0.5, 0.21875, ((0, 64),))
    tile_rows = draw_tile_rows(jax.random.fold_in(streams_of[6], 71), 0)
    tile_srcs = draw_tile_srcs(jax.random.fold_in(streams_of[6], 71), 0)
    send_rows = draw_send_rows(jax.random.fold_in(streams_of[6], 71), 0)
    basis = draw_basis(jax.random.fold_in(streams_of[6], 71), 0)
    rotation = bell_draw(streams_of[5], (K, K), K ** -0.5, 0.375, ((1, 8),))
    return {"tiles": tiles, "tile_rows": tile_rows, "tile_srcs": tile_srcs, "send_rows": send_rows, "basis": basis, "rotation": rotation}


def spread(field, tiles, tile_rows, tile_srcs, send_rows):
    blocks = field.reshape(K, N_DOM, RB, TILE).transpose(1, 0, 2, 3)
    tiles_dev = tiles.reshape(N_DOM, TPD, TILE, TILE)
    rows_dev = tile_rows.reshape(N_DOM, TPD)
    srcs_dev = tile_srcs.reshape(N_DOM, TPD)
    senders = jnp.arange(N_DOM, dtype=jnp.int32)

    def one(device):
        own = blocks[device]
        arrived = blocks[senders, :, send_rows[:, device], :]
        pool = jnp.concatenate([own, arrived.transpose(1, 0, 2)], axis=1)
        sources = jnp.take(pool, srcs_dev[device], axis=1).astype(jnp.float32)
        contrib = jnp.einsum("ktj,tij->kti", sources, tiles_dev[device].astype(jnp.float32), precision=lax.Precision.HIGHEST)
        owner = (rows_dev[device][:, None] == jnp.arange(RB, dtype=jnp.int32)[None, :]).astype(jnp.float32)
        return jnp.einsum("kti,tr->kri", contrib, owner, precision=lax.Precision.HIGHEST)

    out = lax.map(one, jnp.arange(N_DOM, dtype=jnp.int32))
    return out.transpose(1, 0, 2, 3).reshape(K, NROWS).astype(jnp.bfloat16)


def reference(tiles, tile_rows, tile_srcs, send_rows, basis, rotation):
    first = spread(basis, tiles, tile_rows, tile_srcs, send_rows)
    second = spread(first, tiles, tile_rows, tile_srcs, send_rows)
    gram = jnp.dot(second, second.T, preferred_element_type=jnp.float32) / NROWS
    rotated = jnp.dot(rotation.T, second, preferred_element_type=jnp.float32).astype(jnp.bfloat16)
    return gram, rotated
```

```python
import jax
import jax.numpy as jnp
from jax import lax
from jax.experimental import pallas as pl
from jax.experimental.pallas import tpu as pltpu
from jax.sharding import PartitionSpec as P

MESH = pl.DeviceIdType.MESH
TILE = 128
RB = 16
TPD = 96
WIDTH = 32
K = 256
ROWS = RB * TILE
NX, NZ = 4, 16
NDOM = NX * NZ
NY, NCORE = 4, 2
NCOL = NY * NCORE
OWN = TPD - NDOM
GROUP = 4


def dom_at(me, i, sign):
    x, z = me // NZ, me % NZ
    kk = NZ - 1 - i // NX
    dz = jnp.where(kk % 2 == 1, (kk + 1) // 2, NZ - (kk + 1) // 2)
    dx = NX - 1 - i % NX
    return ((x + sign * dx + NX) % NX) * NZ + (z + sign * dz + NZ) % NZ


def loop(lo, hi, body):
    def step(i, carry):
        body(i)
        return carry

    lax.fori_loop(lo, hi, step, 0)


def build_tables(rows, srcs, tab):
    tab[...] = jnp.zeros_like(tab)
    at = lax.broadcasted_iota(jnp.int32, (TPD, TPD), 0)
    other = lax.broadcasted_iota(jnp.int32, (TPD, TPD), 1)
    rows_l = jnp.broadcast_to(rows[...], (TPD, TPD))
    srcs_l = jnp.broadcast_to(srcs[...], (TPD, TPD))

    def along(value):
        return jnp.sum(value, axis=1, keepdims=True)

    def across(value):
        return jnp.sum(value, axis=0, keepdims=True)

    one = jnp.ones((TPD, TPD), jnp.int32)
    zero = jnp.zeros((TPD, TPD), jnp.int32)
    rows_c = along(jnp.where(at == other, rows_l, zero))
    srcs_c = along(jnp.where(at == other, srcs_l, zero))
    earlier = other < at
    own_rank = along(jnp.where(jnp.logical_and(earlier, srcs_l < RB), one, zero))
    slot = jnp.where(srcs_c < RB, jnp.minimum(NDOM + own_rank, TPD - 1), srcs_c - RB)
    same_before = along(jnp.where(jnp.logical_and(rows_l == rows_c, earlier), one, zero))
    place = along(jnp.where(rows_l < rows_c, one, zero)) + same_before
    keep = jnp.minimum(same_before, 1)
    slot_here = slot == other
    place_here = place == other
    def put(n, most, value):
        tab[n : n + 1, 0:TPD] = jnp.minimum(across(value), most)

    put(0, TPD - 1, jnp.where(slot_here, at, zero))
    put(1, RB - 1, jnp.where(slot_here, jnp.broadcast_to(jnp.minimum(srcs_c, RB - 1), (TPD, TPD)), zero))
    put(2, TPD - 1, jnp.where(place_here, jnp.broadcast_to(slot, (TPD, TPD)), zero))
    put(3, 1, jnp.where(place_here, jnp.broadcast_to(keep, (TPD, TPD)), zero))
    upto = across(jnp.where(rows_c <= other, one, zero))
    tab[4:5, 0:TPD] = jnp.maximum(upto - 1, 0)


def kernel(
    tiles_h, rows_h, srcs_h, send_h, basis_h, rot_h,
    gram_ref, out_ref,
    tiles, rows, srcs, send_rows, basis, rot, tab, tabs,
    field, sbuf, rbuf, prods, sums, whole,
    gsend, grecv, gx, gfin,
    in_sem, ssem, rsem, row_sem, csend, crecv, gs1, gr1, gs2, gr2, gs3, gr3,
):
    me, mc = lax.axis_index("dom"), lax.axis_index("col")
    x, z = me // NZ, me % NZ
    y, core = mc // NCORE, mc % NCORE
    bar = pltpu.get_barrier_semaphore()

    loads = [
        pltpu.make_async_copy(src, dst, in_sem.at[n])
        for n, (src, dst) in enumerate(
            ((basis_h, basis), (send_h, send_rows), (rows_h, rows), (srcs_h, srcs), (tiles_h, tiles), (rot_h, rot))
        )
    ]
    for load in loads:
        load.start()

    def z_peer(d):
        return x * NZ + (z + d) % NZ

    def x_peer(d):
        return ((x + d) % NX) * NZ + z

    def y_peer(d):
        return ((y + d) % NY) * NCORE + core

    sibling = y * NCORE + 1 - core

    def greet(sem, **where):
        pl.semaphore_signal(sem, inc=1, device_id=where, device_id_type=MESH)

    for d in range(1, NX):
        greet(bar, dom=x_peer(d))
    loop(1, NZ, lambda d: greet(bar, dom=z_peer(d)))
    for d in range(1, NY):
        greet(bar, col=y_peer(d))
    greet(bar, col=sibling)

    for n in range(2):
        loads[n].wait()
    for r in range(RB):
        field[r] = basis[:, r * TILE : (r + 1) * TILE]

    pl.semaphore_wait(bar, NX - 1 + NZ - 1 + NY)
    for d in range(1, NX):
        greet(row_sem, dom=x_peer(d))
    pl.semaphore_wait(row_sem, NX - 1)

    def halo(p, peer, slot):
        return pltpu.make_async_remote_copy(
            src_ref=sbuf.at[p, peer], dst_ref=rbuf.at[p, slot],
            send_sem=ssem.at[p, peer], recv_sem=rsem.at[p, slot],
            device_id={"dom": peer}, device_id_type=MESH,
        )

    def product(block, tile):
        return lax.dot_general(block, tile, (((1,), (1,)), ((), ())), preferred_element_type=jnp.float32)

    for p in range(2):

        def send(i):
            peer = dom_at(me, i, 1)
            sbuf[p, peer] = field[send_rows[0, peer]]
            halo(p, peer, me).start()

        loop(0, NDOM - 1, send)
        rbuf[p, me] = field[send_rows[0, me]]

        if p == 0:
            for n in range(2, 5):
                loads[n].wait()
            build_tables(rows, srcs, tab)
            to_smem = pltpu.make_async_copy(tab, tabs, in_sem.at[6])
            to_smem.start()
            to_smem.wait()

        def own(g):
            for u in range(GROUP):
                s = NDOM + g * GROUP + u
                prods[s] = product(field[tabs[1, s]], tiles[tabs[0, s]])

        loop(0, OWN // GROUP, own)

        def received(g):
            origins = [dom_at(me, g * GROUP + u, -1) for u in range(GROUP)]
            for origin in origins:
                halo(p, origin, origin).wait_recv()
            for origin in origins:
                prods[origin] = product(rbuf[p, origin], tiles[tabs[0, origin]])

        loop(0, NDOM // GROUP - 1, received)
        last = [dom_at(me, NDOM - GROUP + u, -1) for u in range(GROUP)]
        for origin in last[:-1]:
            halo(p, origin, origin).wait_recv()
        for origin in last:
            prods[origin] = product(rbuf[p, origin], tiles[tabs[0, origin]])

        def running(g, acc):
            for u in range(GROUP):
                s = g * GROUP + u
                acc = jnp.where(tabs[3, s] > 0, acc, 0.0) + prods[tabs[2, s]]
                sums[s] = acc
            return acc

        lax.fori_loop(0, TPD // GROUP, running, jnp.zeros((WIDTH, TILE), jnp.float32))
        for r in range(RB):
            block = sums[tabs[4, r]].astype(jnp.bfloat16)
            if p == 0:
                field[r] = block
            else:
                whole[pl.ds(pl.multiple_of(mc * WIDTH, WIDTH), WIDTH), r * TILE : (r + 1) * TILE] = block

    def part(owner):
        return whole.at[pl.ds(pl.multiple_of(owner * WIDTH, WIDTH), WIDTH)]

    def pass_on(owner, to, n):
        return pltpu.make_async_remote_copy(
            src_ref=part(owner), dst_ref=part(owner), send_sem=csend.at[n], recv_sem=crecv.at[n],
            device_id={"col": to}, device_id_type=MESH,
        )

    outward = [pass_on(mc, y_peer(d), d) for d in (2, 1, 3)] + [pass_on(mc, sibling, 0)]
    for copy in outward:
        copy.start()
    loads[5].wait()
    rotation = rot[...].T
    onward = []
    for d in (1, 3, 2):
        origin = y_peer(NY - d)
        pass_on(origin, mc, d).wait_recv()
        copy = pass_on(origin, sibling, NY + d)
        copy.start()
        onward.append(copy)
    pass_on(sibling, mc, 0).wait_recv()
    for d in (1, 3, 2):
        pass_on(((y + NY - d) % NY) * NCORE + 1 - core, mc, NY + d).wait_recv()

    gram = lax.dot_general(
        part(mc)[...], whole[...], (((1,), (1,)), ((), ())), preferred_element_type=jnp.float32
    ) * (1.0 / (ROWS * NDOM))
    for k in range(NZ):
        gsend[k, 0:2] = gram[2 * k : 2 * k + 2, 0:TILE]
        gsend[k, 2:4] = gram[2 * k : 2 * k + 2, TILE : 2 * TILE]

    def gram_out(d, sign):
        to = (z + sign * d + NZ) % NZ
        return pltpu.make_async_remote_copy(
            src_ref=gsend.at[to], dst_ref=grecv.at[z], send_sem=gs1.at[d], recv_sem=gr1.at[d],
            device_id={"dom": x * NZ + to}, device_id_type=MESH,
        )

    loop(1, NZ, lambda d: gram_out(d, 1).start())
    grecv[z] = gsend[z]

    def rotate(c):
        cols = pl.ds(pl.multiple_of(c * 512, 512), 512)
        out_ref[:, cols] = jnp.dot(rotation, whole[:, cols], preferred_element_type=jnp.float32).astype(jnp.bfloat16)

    loop(0, ROWS // 512, rotate)

    loop(1, NZ, lambda d: gram_out(d, -1).wait_recv())
    total = grecv[0]
    for k in range(1, NZ):
        total = total + grecv[k]
    gx[x] = total

    def gram_x(d):
        return pltpu.make_async_remote_copy(
            src_ref=gx.at[x], dst_ref=gx.at[x], send_sem=gs2.at[d], recv_sem=gr2.at[d],
            device_id={"dom": x_peer(d)}, device_id_type=MESH,
        )

    def gram_x_from(d):
        origin = (x + NX - d) % NX
        return pltpu.make_async_remote_copy(
            src_ref=gx.at[origin], dst_ref=gx.at[origin], send_sem=gs2.at[d], recv_sem=gr2.at[d],
            device_id={"dom": x_peer(d)}, device_id_type=MESH,
        )

    for d in range(1, NX):
        gram_x(d).start()
    for d in range(1, NX):
        gram_x_from(d).wait_recv()
    gfin[z] = ((gx[0] + gx[1]) + gx[2]) + gx[3]

    def gram_back(owner, d):
        return pltpu.make_async_remote_copy(
            src_ref=gfin.at[owner], dst_ref=gfin.at[owner], send_sem=gs3.at[d], recv_sem=gr3.at[d],
            device_id={"dom": z_peer(d)}, device_id_type=MESH,
        )

    loop(1, NZ, lambda d: gram_back(z, d).start())
    loop(1, NZ, lambda d: gram_back((z + NZ - d) % NZ, d).wait_recv())
    for half in range(2):
        rows_of = jnp.concatenate([gfin[k, 2 * half : 2 * half + 2] for k in range(NZ)], axis=0)
        gram_ref[half * TILE : (half + 1) * TILE, :] = rows_of.T

    for p in range(2):
        loop(0, NDOM - 1, lambda i: halo(p, dom_at(me, i, 1), me).wait_send())
    for copy in outward + onward:
        copy.wait_send()
    loop(1, NZ, lambda d: gram_out(d, 1).wait_send())
    for d in range(1, NX):
        gram_x(d).wait_send()
    loop(1, NZ, lambda d: gram_back(z, d).wait_send())


def per_device(tiles, tile_rows, tile_srcs, send_rows, basis, rotation):
    any_space = pl.BlockSpec(memory_space=pl.ANY)
    vmem = pl.BlockSpec(memory_space=pltpu.VMEM)
    dma = pltpu.SemaphoreType.DMA
    return pl.pallas_call(
        kernel,
        out_shape=(
            jax.ShapeDtypeStruct((K, WIDTH), jnp.float32),
            jax.ShapeDtypeStruct((WIDTH, ROWS), jnp.bfloat16),
        ),
        in_specs=[any_space] * 6,
        out_specs=(vmem, vmem),
        scratch_shapes=[
            pltpu.VMEM((TPD, TILE, TILE), jnp.bfloat16),
            pltpu.VMEM((1, TPD), jnp.int32),
            pltpu.VMEM((1, TPD), jnp.int32),
            pltpu.SMEM((1, NDOM), jnp.int32),
            pltpu.VMEM((WIDTH, ROWS), jnp.bfloat16),
            pltpu.VMEM((K, WIDTH), jnp.bfloat16),
            pltpu.VMEM((8, 128), jnp.int32),
            pltpu.SMEM((8, 128), jnp.int32),
            pltpu.VMEM((RB, WIDTH, TILE), jnp.bfloat16),
            pltpu.VMEM((2, NDOM, WIDTH, TILE), jnp.bfloat16),
            pltpu.VMEM((2, NDOM, WIDTH, TILE), jnp.bfloat16),
            pltpu.VMEM((TPD, WIDTH, TILE), jnp.float32),
            pltpu.VMEM((TPD, WIDTH, TILE), jnp.float32),
            pltpu.VMEM((K, ROWS), jnp.bfloat16),
            pltpu.VMEM((NZ, 4, TILE), jnp.float32),
            pltpu.VMEM((NZ, 4, TILE), jnp.float32),
            pltpu.VMEM((NX, 4, TILE), jnp.float32),
            pltpu.VMEM((NZ, 4, TILE), jnp.float32),
            dma((7,)),
            dma((2, NDOM)),
            dma((2, NDOM)),
            pltpu.SemaphoreType.REGULAR,
            dma((2 * NY,)),
            dma((2 * NY,)),
            dma((NZ,)),
            dma((NZ,)),
            dma((NX,)),
            dma((NX,)),
            dma((NZ,)),
            dma((NZ,)),
        ],
        compiler_params=pltpu.CompilerParams(collective_id=0, has_side_effects=True, vmem_limit_bytes=56 << 20),
        cost_estimate=pl.CostEstimate(flops=300_000_000, bytes_accessed=4 << 20, transcendentals=0),
    )(tiles, tile_rows.reshape(1, TPD), tile_srcs.reshape(1, TPD), send_rows, basis, rotation)


def solution(mesh):
    return jax.shard_map(
        per_device,
        mesh=mesh,
        in_specs=(
            P("dom", None, None),
            P("dom"),
            P("dom"),
            P("dom", None),
            P("col", "dom"),
            P(None, "col"),
        ),
        out_specs=(P(None, "col"), P("col", "dom")),
        check_vma=False,
    )
```

```python
import jax
import jax.numpy as jnp
from jax import lax
from jax.experimental import pallas as pl
from jax.experimental.pallas import tpu as pltpu
from jax.sharding import PartitionSpec as P

MESH = pl.DeviceIdType.MESH
TILE = 128
RB = 16
TPD = 96
WIDTH = 32
K = 256
ROWS = RB * TILE
NX, NZ = 4, 16
NDOM = NX * NZ
NY, NCORE = 4, 2
NCOL = NY * NCORE
OWN = TPD - NDOM
GROUP = 4
HALF = NZ // 2
HALVES = 2
PART = WIDTH // HALVES
CHUNK = WIDTH // NX


def loop(lo, hi, body):
    def step(i, carry):
        body(i)
        return carry

    lax.fori_loop(lo, hi, step, 0)


def build_tables(rows, srcs, tab):
    tab[...] = jnp.zeros_like(tab)
    at = lax.broadcasted_iota(jnp.int32, (TPD, TPD), 0)
    other = lax.broadcasted_iota(jnp.int32, (TPD, TPD), 1)
    rows_l = jnp.broadcast_to(rows[...], (TPD, TPD))
    srcs_l = jnp.broadcast_to(srcs[...], (TPD, TPD))

    def along(value):
        return jnp.sum(value, axis=1, keepdims=True)

    def across(value):
        return jnp.sum(value, axis=0, keepdims=True)

    one = jnp.ones((TPD, TPD), jnp.int32)
    zero = jnp.zeros((TPD, TPD), jnp.int32)
    rows_c = along(jnp.where(at == other, rows_l, zero))
    srcs_c = along(jnp.where(at == other, srcs_l, zero))
    earlier = other < at
    own_rank = along(jnp.where(jnp.logical_and(earlier, srcs_l < RB), one, zero))
    slot = jnp.where(srcs_c < RB, jnp.minimum(NDOM + own_rank, TPD - 1), srcs_c - RB)
    same_before = along(jnp.where(jnp.logical_and(rows_l == rows_c, earlier), one, zero))
    place = along(jnp.where(rows_l < rows_c, one, zero)) + same_before
    keep = jnp.minimum(same_before, 1)
    slot_here = slot == other
    place_here = place == other
    def put(n, most, value):
        tab[n : n + 1, 0:TPD] = jnp.minimum(across(value), most)

    put(0, TPD - 1, jnp.where(slot_here, at, zero))
    put(1, RB - 1, jnp.where(slot_here, jnp.broadcast_to(jnp.minimum(srcs_c, RB - 1), (TPD, TPD)), zero))
    put(2, TPD - 1, jnp.where(place_here, jnp.broadcast_to(slot, (TPD, TPD)), zero))
    put(3, 1, jnp.where(place_here, jnp.broadcast_to(keep, (TPD, TPD)), zero))
    upto = across(jnp.where(rows_c <= other, one, zero))
    tab[4:5, 0:TPD] = jnp.maximum(upto - 1, 0)


def kernel(
    tiles_h, rows_h, srcs_h, send_h, basis_h, rot_h,
    gram_ref, out_ref,
    tiles, rows, srcs, send_rows, basis, rot, tab, tabs,
    field, sbuf, rbuf, prods, sums, whole,
    gpart, gx, gsum, gz,
    in_sem, ssem, rsem, csend, crecv, gs1, gr1, gs2, gr2, gs3, gr3,
):
    me, mc = lax.axis_index("dom"), lax.axis_index("col")
    x, z = lax.div(me, NZ), lax.rem(me, NZ)
    y, core = lax.div(mc, NCORE), lax.rem(mc, NCORE)
    lines_to = [lax.rem(x + dx, NX) * NZ for dx in range(NX)]
    lines_from = [lax.rem(x + NX - dx, NX) * NZ for dx in range(NX)]

    def targets(j):
        ahead = (lax.rem(z + HALF + j, NZ), lax.rem(z + HALF - 1 - j, NZ))
        return [line + at for at in ahead for line in lines_to[::-1]]

    def origins(j):
        behind = (lax.rem(z + HALF - j, NZ), lax.rem(z + HALF + 1 + j, NZ))
        return [line + at for at in behind for line in lines_from[::-1]]

    def over_peers(body):
        loop(0, HALF - 1, lambda j: body(j, 2 * NX))
        body(HALF - 1, 2 * NX - 1)
    bar = pltpu.get_barrier_semaphore()

    loads = [
        pltpu.make_async_copy(src, dst, in_sem.at[n])
        for n, (src, dst) in enumerate(
            ((basis_h, basis), (send_h, send_rows), (rows_h, rows), (srcs_h, srcs), (tiles_h, tiles), (rot_h, rot))
        )
    ]
    for load in loads:
        load.start()

    def y_peer(d):
        return ((y + d) % NY) * NCORE + core

    sibling = y * NCORE + 1 - core

    def greet(**where):
        pl.semaphore_signal(bar, inc=1, device_id=where, device_id_type=MESH)

    def greet_peers(j, most):
        for peer in targets(j)[:most]:
            greet(dom=peer)

    over_peers(greet_peers)
    for d in range(1, NY):
        greet(col=y_peer(d))
    greet(col=sibling)

    for n in range(2):
        loads[n].wait()
    for h in range(HALVES):
        for r in range(RB):
            field[h, r] = basis[h * PART : (h + 1) * PART, r * TILE : (r + 1) * TILE]

    pl.semaphore_wait(bar, NDOM - 1 + NY)

    def halo(p, h, peer, slot):
        return pltpu.make_async_remote_copy(
            src_ref=sbuf.at[p, h, peer], dst_ref=rbuf.at[p, h, slot],
            send_sem=ssem.at[p, h, peer], recv_sem=rsem.at[p, h, slot],
            device_id={"dom": peer}, device_id_type=MESH,
        )

    def product(block, tile):
        return lax.dot_general(block, tile, (((1,), (1,)), ((), ())), preferred_element_type=jnp.float32)

    def send(p, h):
        def some(j, most):
            peers = targets(j)
            for peer in peers[:most]:
                sbuf[p, h, peer] = field[h, send_rows[0, peer]]
            for peer in peers[:most]:
                halo(p, h, peer, me).start()

        over_peers(some)
        rbuf[p, h, me] = field[h, send_rows[0, me]]

    def send_ended(p, h):
        def some(j, most):
            for peer in targets(j)[:most]:
                halo(p, h, peer, me).wait_send()

        over_peers(some)

    def own(h):
        def group(g):
            for u in range(GROUP):
                s = NDOM + g * GROUP + u
                prods[h, s] = product(field[h, tabs[1, s]], tiles[tabs[0, s]])

        loop(0, OWN // GROUP, group)

    def receive(p, h, first, past):
        def take(j, waits):
            peers = origins(j)
            for peer in peers[:waits]:
                halo(p, h, peer, peer).wait_recv()
            for peer in peers:
                prods[h, peer] = product(rbuf[p, h, peer], tiles[tabs[0, peer]])

        loop(first, min(past, HALF - 1), lambda j: take(j, 2 * NX))
        if past == HALF:
            take(HALF - 1, 2 * NX - 1)

    def add_up(h):
        def running(g, acc):
            for u in range(GROUP):
                s = g * GROUP + u
                acc = jnp.where(tabs[3, s] > 0, acc, 0.0) + prods[h, tabs[2, s]]
                sums[s] = acc
            return acc

        lax.fori_loop(0, TPD // GROUP, running, jnp.zeros((PART, TILE), jnp.float32))
        return [sums[tabs[4, r]].astype(jnp.bfloat16) for r in range(RB)]

    def part(owner, h):
        return whole.at[pl.ds(pl.multiple_of(owner * WIDTH + h * PART, PART), PART)]

    def pass_on(owner, h, to, n):
        return pltpu.make_async_remote_copy(
            src_ref=part(owner, h), dst_ref=part(owner, h), send_sem=csend.at[h, n], recv_sem=crecv.at[h, n],
            device_id={"col": to}, device_id_type=MESH,
        )

    sent = []

    def begin(copy):
        copy.start()
        sent.append(copy)

    def spread_out(h):
        for d in (2, 1, 3):
            begin(pass_on(mc, h, y_peer(d), d))
        begin(pass_on(mc, h, sibling, 0))

    def hand_over(h):
        for d in (1, 3, 2):
            origin = y_peer(NY - d)
            pass_on(origin, h, mc, d).wait_recv()
            begin(pass_on(origin, h, sibling, NY + d))

    def gathered(h):
        pass_on(sibling, h, mc, 0).wait_recv()
        for d in (1, 3, 2):
            pass_on(((y + NY - d) % NY) * NCORE + 1 - core, h, mc, NY + d).wait_recv()

    def first_done(h):
        for r, block in enumerate(add_up(h)):
            field[h, r] = block

    def second_done(h):
        mine = pl.ds(pl.multiple_of(mc * WIDTH + h * PART, PART), PART)
        for r, block in enumerate(add_up(h)):
            whole[mine, r * TILE : (r + 1) * TILE] = block

    for h in range(HALVES):
        send(0, h)
    for n in range(2, 5):
        loads[n].wait()
    build_tables(rows, srcs, tab)
    to_smem = pltpu.make_async_copy(tab, tabs, in_sem.at[6])
    to_smem.start()
    to_smem.wait()
    for h in range(HALVES):
        own(h)
    for h in range(HALVES):
        receive(0, h, 0, HALF)
        first_done(h)
        send(1, h)
        own(h)
    for h in range(HALVES):
        receive(1, h, 0, HALF - 2)
        if h > 0:
            hand_over(h - 1)
        receive(1, h, HALF - 2, HALF)
        second_done(h)
        spread_out(h)
    loads[5].wait()
    for h in range(HALVES - 1):
        gathered(h)
    hand_over(HALVES - 1)
    gathered(HALVES - 1)

    mine = pl.ds(pl.multiple_of(mc * WIDTH, WIDTH), WIDTH)
    gram = lax.dot_general(
        whole[mine, :], whole[...], (((1,), (1,)), ((), ())), preferred_element_type=jnp.float32
    ) * (1.0 / (ROWS * NDOM))
    for k in range(NX):
        gpart[k] = gram[k * CHUNK : (k + 1) * CHUNK, :]

    def x_scatter(d, sign):
        to = (x + sign * d + NX) % NX
        return pltpu.make_async_remote_copy(
            src_ref=gpart.at[to], dst_ref=gx.at[x], send_sem=gs1.at[d], recv_sem=gr1.at[d],
            device_id={"dom": to * NZ + z}, device_id_type=MESH,
        )

    for d in range(1, NX):
        x_scatter(d, 1).start()
    gx[x] = gpart[x]
    for d in range(1, NX):
        x_scatter(d, -1).wait_recv()
    gz[z] = ((gx[0] + gx[1]) + gx[2]) + gx[3]

    def z_share(owner, d):
        return pltpu.make_async_remote_copy(
            src_ref=gz.at[owner], dst_ref=gz.at[owner], send_sem=gs2.at[d], recv_sem=gr2.at[d],
            device_id={"dom": x * NZ + (z + d) % NZ}, device_id_type=MESH,
        )

    z_order = sorted(range(1, NZ), key=lambda d: -min(d, NZ - d))
    for d in z_order:
        z_share(z, d).start()

    def rotate(c):
        cols = pl.ds(pl.multiple_of(c * 512, 512), 512)
        out_ref[:, cols] = jnp.dot(rot[...], whole[:, cols], preferred_element_type=jnp.float32).astype(jnp.bfloat16)

    loop(0, ROWS // 512, rotate)
    for d in z_order:
        z_share((z + NZ - d) % NZ, d).wait_recv()
    total = gz[0]
    for k in range(1, NZ):
        total = total + gz[k]
    gsum[x] = total

    def x_share(owner, d):
        return pltpu.make_async_remote_copy(
            src_ref=gsum.at[owner], dst_ref=gsum.at[owner], send_sem=gs3.at[d], recv_sem=gr3.at[d],
            device_id={"dom": ((x + d) % NX) * NZ + z}, device_id_type=MESH,
        )

    for d in range(1, NX):
        x_share(x, d).start()
    for p in range(2):
        for h in range(HALVES):
            send_ended(p, h)
    for copy in sent:
        copy.wait_send()
    for d in range(1, NX):
        x_scatter(d, 1).wait_send()
    for d in range(1, NZ):
        z_share(z, d).wait_send()
    for d in range(1, NX):
        x_share((x + NX - d) % NX, d).wait_recv()
    for k in range(NX):
        gram_ref[k * CHUNK : (k + 1) * CHUNK, :] = gsum[k]
    for d in range(1, NX):
        x_share(x, d).wait_send()


def per_device(tiles, tile_rows, tile_srcs, send_rows, basis, rotation):
    any_space = pl.BlockSpec(memory_space=pl.ANY)
    vmem = pl.BlockSpec(memory_space=pltpu.VMEM)
    dma = pltpu.SemaphoreType.DMA
    gram, rotated = pl.pallas_call(
        kernel,
        out_shape=(
            jax.ShapeDtypeStruct((WIDTH, K), jnp.float32),
            jax.ShapeDtypeStruct((WIDTH, ROWS), jnp.bfloat16),
        ),
        in_specs=[any_space] * 6,
        out_specs=(vmem, vmem),
        scratch_shapes=[
            pltpu.VMEM((TPD, TILE, TILE), jnp.bfloat16),
            pltpu.VMEM((1, TPD), jnp.int32),
            pltpu.VMEM((1, TPD), jnp.int32),
            pltpu.SMEM((1, NDOM), jnp.int32),
            pltpu.VMEM((WIDTH, ROWS), jnp.bfloat16),
            pltpu.VMEM((WIDTH, K), jnp.bfloat16),
            pltpu.VMEM((8, 128), jnp.int32),
            pltpu.SMEM((8, 128), jnp.int32),
            pltpu.VMEM((HALVES, RB, PART, TILE), jnp.bfloat16),
            pltpu.VMEM((2, HALVES, NDOM, PART, TILE), jnp.bfloat16),
            pltpu.VMEM((2, HALVES, NDOM, PART, TILE), jnp.bfloat16),
            pltpu.VMEM((HALVES, TPD, PART, TILE), jnp.float32),
            pltpu.VMEM((TPD, PART, TILE), jnp.float32),
            pltpu.VMEM((K, ROWS), jnp.bfloat16),
            pltpu.VMEM((NX, CHUNK, K), jnp.float32),
            pltpu.VMEM((NX, CHUNK, K), jnp.float32),
            pltpu.VMEM((NX, CHUNK, K), jnp.float32),
            pltpu.VMEM((NZ, CHUNK, K), jnp.float32),
            dma((7,)),
            dma((2, HALVES, NDOM)),
            dma((2, HALVES, NDOM)),
            dma((HALVES, 2 * NY)),
            dma((HALVES, 2 * NY)),
            dma((NX,)),
            dma((NX,)),
            dma((NZ,)),
            dma((NZ,)),
            dma((NX,)),
            dma((NX,)),
        ],
        compiler_params=pltpu.CompilerParams(collective_id=0, has_side_effects=True, vmem_limit_bytes=56 << 20),
        cost_estimate=pl.CostEstimate(flops=300_000_000, bytes_accessed=4 << 20, transcendentals=0),
    )(tiles, tile_rows.reshape(1, TPD), tile_srcs.reshape(1, TPD), send_rows, basis, rotation.T)
    return gram.T, rotated


def solution(mesh):
    return jax.shard_map(
        per_device,
        mesh=mesh,
        in_specs=(
            P("dom", None, None),
            P("dom"),
            P("dom"),
            P("dom", None),
            P("col", "dom"),
            P(None, "col"),
        ),
        out_specs=(P(None, "col"), P("col", "dom")),
        check_vma=False,
    )
```

```python
import jax
import jax.numpy as jnp
from jax import lax
from jax.experimental import pallas as pl
from jax.experimental.pallas import tpu as pltpu
from jax.sharding import PartitionSpec as P

MESH = pl.DeviceIdType.MESH
TILE = 128
RB = 16
TPD = 96
WIDTH = 32
K = 256
ROWS = RB * TILE
NX, NZ = 4, 16
NDOM = NX * NZ
NY, NCORE = 4, 2
NCOL = NY * NCORE
OWN = TPD - NDOM
GROUP = 4
HALF = NZ // 2
BATCH = 2 * NX
HALVES = 2
PART = WIDTH // HALVES
CHUNK = WIDTH // NX


def loop(lo, hi, body):
    def step(i, carry):
        body(i)
        return carry

    lax.fori_loop(lo, hi, step, 0)


def build_tables(rows, srcs, tab):
    tab[...] = jnp.zeros_like(tab)
    at = lax.broadcasted_iota(jnp.int32, (TPD, TPD), 0)
    other = lax.broadcasted_iota(jnp.int32, (TPD, TPD), 1)
    rows_l = jnp.broadcast_to(rows[...], (TPD, TPD))
    srcs_l = jnp.broadcast_to(srcs[...], (TPD, TPD))

    def along(value):
        return jnp.sum(value, axis=1, keepdims=True)

    def across(value):
        return jnp.sum(value, axis=0, keepdims=True)

    one = jnp.ones((TPD, TPD), jnp.int32)
    zero = jnp.zeros((TPD, TPD), jnp.int32)
    rows_c = along(jnp.where(at == other, rows_l, zero))
    srcs_c = along(jnp.where(at == other, srcs_l, zero))
    earlier = other < at
    own_rank = along(jnp.where(jnp.logical_and(earlier, srcs_l < RB), one, zero))
    slot = jnp.where(srcs_c < RB, jnp.minimum(NDOM + own_rank, TPD - 1), srcs_c - RB)
    same_before = along(jnp.where(jnp.logical_and(rows_l == rows_c, earlier), one, zero))
    place = along(jnp.where(rows_l < rows_c, one, zero)) + same_before
    keep = jnp.minimum(same_before, 1)
    slot_here = slot == other
    place_here = place == other
    def put(n, most, value):
        tab[n : n + 1, 0:TPD] = jnp.minimum(across(value), most)

    put(0, TPD - 1, jnp.where(slot_here, at, zero))
    put(1, RB - 1, jnp.where(slot_here, jnp.broadcast_to(jnp.minimum(srcs_c, RB - 1), (TPD, TPD)), zero))
    put(2, TPD - 1, jnp.where(place_here, jnp.broadcast_to(slot, (TPD, TPD)), zero))
    put(3, 1, jnp.where(place_here, jnp.broadcast_to(keep, (TPD, TPD)), zero))
    upto = across(jnp.where(rows_c <= other, one, zero))
    tab[4:5, 0:TPD] = jnp.maximum(upto - 1, 0)


def kernel(
    tiles_h, rows_h, srcs_h, send_h, basis_h, rot_h,
    gram_ref, out_ref,
    tiles, rows, srcs, send_rows, basis, rot, tab, tabs,
    field, sbuf, rbuf, prods, sums, whole,
    gpart, gx, gsum, gz,
    in_sem, ssem, rsem, csend, crecv, gsem,
):
    me, mc = lax.axis_index("dom"), lax.axis_index("col")
    x, z = lax.div(me, NZ), lax.rem(me, NZ)
    y, core = lax.div(mc, NCORE), lax.rem(mc, NCORE)
    lines_to = [lax.rem(x + dx, NX) * NZ for dx in range(NX)]
    lines_from = [lax.rem(x + NX - dx, NX) * NZ for dx in range(NX)]

    def targets(j):
        ahead = (lax.rem(z + HALF + j, NZ), lax.rem(z + HALF - 1 - j, NZ))
        return [line + at for at in ahead for line in lines_to[::-1]]

    def origins(j):
        behind = (lax.rem(z + HALF - j, NZ), lax.rem(z + HALF + 1 + j, NZ))
        return [line + at for at in behind for line in lines_from[::-1]]

    def over_peers(body):
        loop(0, HALF - 1, lambda j: body(j, BATCH))
        body(HALF - 1, BATCH - 1)
    bar = pltpu.get_barrier_semaphore()

    loads = [
        pltpu.make_async_copy(src, dst, in_sem.at[n])
        for n, (src, dst) in enumerate(
            ((basis_h, basis), (send_h, send_rows), (rows_h, rows), (srcs_h, srcs), (tiles_h, tiles), (rot_h, rot))
        )
    ]
    for load in loads:
        load.start()

    def y_peer(d):
        return ((y + d) % NY) * NCORE + core

    sibling = y * NCORE + 1 - core

    def greet(**where):
        pl.semaphore_signal(bar, inc=1, device_id=where, device_id_type=MESH)

    def greet_peers(j, most):
        for peer in targets(j)[:most]:
            greet(dom=peer)

    over_peers(greet_peers)
    for d in range(1, NY):
        greet(col=y_peer(d))
    greet(col=sibling)

    for n in range(2):
        loads[n].wait()
    for h in range(HALVES):
        for r in range(RB):
            field[h, r] = basis[h * PART : (h + 1) * PART, r * TILE : (r + 1) * TILE]

    pl.semaphore_wait(bar, NDOM - 1 + NY)

    def halo(p, h, j, u, peer):
        slot = j * BATCH + u
        return pltpu.make_async_remote_copy(
            src_ref=sbuf.at[p, h, slot], dst_ref=rbuf.at[p, h, slot], send_sem=ssem.at[p, h], recv_sem=rsem.at[p, h, j],
            device_id={"dom": peer}, device_id_type=MESH,
        )

    def halo_batch(p, h, j, first, count):
        slots = pl.ds(first, count)
        return pltpu.make_async_remote_copy(
            src_ref=sbuf.at[p, h, slots], dst_ref=rbuf.at[p, h, slots], send_sem=ssem.at[p, h], recv_sem=rsem.at[p, h, j],
            device_id={"dom": x * NZ + lax.rem(z + 1, NZ)}, device_id_type=MESH,
        )

    def product(block, tile):
        return lax.dot_general(block, tile, (((1,), (1,)), ((), ())), preferred_element_type=jnp.float32)

    def send(p, h):
        def some(j, most):
            peers = targets(j)
            for u, peer in enumerate(peers[:most]):
                sbuf[p, h, j * BATCH + u] = field[h, send_rows[0, peer]]
            for u, peer in enumerate(peers[:most]):
                halo(p, h, j, u, peer).start()

        over_peers(some)
        rbuf[p, h, NDOM - 1] = field[h, send_rows[0, me]]

    def own(h):
        def group(g):
            for u in range(GROUP):
                s = NDOM + g * GROUP + u
                prods[h, s] = product(field[h, tabs[1, s]], tiles[tabs[0, s]])

        loop(0, OWN // GROUP, group)

    def receive(p, h, first, past):
        def take(j, waits):
            halo_batch(p, h, j, j * BATCH, waits).wait_recv()
            for u, peer in enumerate(origins(j)):
                prods[h, peer] = product(rbuf[p, h, j * BATCH + u], tiles[tabs[0, peer]])

        loop(first, min(past, HALF - 1), lambda j: take(j, BATCH))
        if past == HALF:
            take(HALF - 1, BATCH - 1)

    def add_up(h):
        def running(g, acc):
            for u in range(GROUP):
                s = g * GROUP + u
                acc = jnp.where(tabs[3, s] > 0, acc, 0.0) + prods[h, tabs[2, s]]
                sums[s] = acc
            return acc

        lax.fori_loop(0, TPD // GROUP, running, jnp.zeros((PART, TILE), jnp.float32))
        return [sums[tabs[4, r]].astype(jnp.bfloat16) for r in range(RB)]

    def part(owner, h):
        return whole.at[pl.ds(pl.multiple_of(owner * WIDTH + h * PART, PART), PART)]

    def pass_on(owner, h, to, n):
        return pltpu.make_async_remote_copy(
            src_ref=part(owner, h), dst_ref=part(owner, h), send_sem=csend.at[h], recv_sem=crecv.at[h, n],
            device_id={"col": to}, device_id_type=MESH,
        )

    def spread_out(h):
        for d in (2, 1, 3):
            pass_on(mc, h, y_peer(d), d).start()
        pass_on(mc, h, sibling, 0).start()

    def hand_over(h):
        for d in (1, 3, 2):
            origin = y_peer(NY - d)
            pass_on(origin, h, mc, d).wait_recv()
            pass_on(origin, h, sibling, NY + d).start()

    def gathered(h):
        pass_on(sibling, h, mc, 0).wait_recv()
        for d in (1, 3, 2):
            pass_on(((y + NY - d) % NY) * NCORE + 1 - core, h, mc, NY + d).wait_recv()

    def first_done(h):
        for r, block in enumerate(add_up(h)):
            field[h, r] = block

    def second_done(h):
        mine = pl.ds(pl.multiple_of(mc * WIDTH + h * PART, PART), PART)
        for r, block in enumerate(add_up(h)):
            whole[mine, r * TILE : (r + 1) * TILE] = block

    for h in range(HALVES):
        send(0, h)
    for n in range(2, 5):
        loads[n].wait()
    build_tables(rows, srcs, tab)
    to_smem = pltpu.make_async_copy(tab, tabs, in_sem.at[6])
    to_smem.start()
    to_smem.wait()
    for h in range(HALVES):
        own(h)
    for h in range(HALVES):
        receive(0, h, 0, HALF)
        first_done(h)
        send(1, h)
        own(h)
    for h in range(HALVES):
        receive(1, h, 0, HALF - 2)
        if h > 0:
            hand_over(h - 1)
        receive(1, h, HALF - 2, HALF)
        second_done(h)
        spread_out(h)
    loads[5].wait()
    for h in range(HALVES - 1):
        gathered(h)
    hand_over(HALVES - 1)
    gathered(HALVES - 1)

    mine = pl.ds(pl.multiple_of(mc * WIDTH, WIDTH), WIDTH)
    gram = lax.dot_general(
        whole[mine, :], whole[...], (((1,), (1,)), ((), ())), preferred_element_type=jnp.float32
    ) * (1.0 / (ROWS * NDOM))
    for k in range(NX):
        gpart[k] = gram[k * CHUNK : (k + 1) * CHUNK, :]

    def batch(ref, count, n):
        return pltpu.make_async_remote_copy(
            src_ref=ref.at[pl.ds(0, count)], dst_ref=ref.at[pl.ds(0, count)], send_sem=gsem.at[n], recv_sem=gsem.at[n + 1],
            device_id={"col": sibling}, device_id_type=MESH,
        )

    def x_scatter(d, sign):
        to = (x + sign * d + NX) % NX
        return pltpu.make_async_remote_copy(
            src_ref=gpart.at[to], dst_ref=gx.at[x], send_sem=gsem.at[0], recv_sem=gsem.at[1],
            device_id={"dom": to * NZ + z}, device_id_type=MESH,
        )

    for d in range(1, NX):
        x_scatter(d, 1).start()
    gx[x] = gpart[x]
    batch(gx, NX - 1, 0).wait_recv()
    gz[z] = ((gx[0] + gx[1]) + gx[2]) + gx[3]

    def z_share(owner, d):
        return pltpu.make_async_remote_copy(
            src_ref=gz.at[owner], dst_ref=gz.at[owner], send_sem=gsem.at[2], recv_sem=gsem.at[3],
            device_id={"dom": x * NZ + (z + d) % NZ}, device_id_type=MESH,
        )

    z_order = sorted(range(1, NZ), key=lambda d: -min(d, NZ - d))
    for d in z_order:
        z_share(z, d).start()

    def rotate(c):
        cols = pl.ds(pl.multiple_of(c * 512, 512), 512)
        out_ref[:, cols] = jnp.dot(rot[...], whole[:, cols], preferred_element_type=jnp.float32).astype(jnp.bfloat16)

    loop(0, ROWS // 512, rotate)
    batch(gz, NZ - 1, 2).wait_recv()
    total = gz[0]
    for k in range(1, NZ):
        total = total + gz[k]
    gsum[x] = total

    def x_share(owner, d):
        return pltpu.make_async_remote_copy(
            src_ref=gsum.at[owner], dst_ref=gsum.at[owner], send_sem=gsem.at[4], recv_sem=gsem.at[5],
            device_id={"dom": ((x + d) % NX) * NZ + z}, device_id_type=MESH,
        )

    for d in range(1, NX):
        x_share(x, d).start()
    for p in range(2):
        for h in range(HALVES):
            halo_batch(p, h, 0, 0, NDOM - 1).wait_send()
    for h in range(HALVES):
        seven = whole.at[pl.ds(0, (2 * NY - 1) * PART)]
        pltpu.make_async_remote_copy(
            src_ref=seven, dst_ref=seven, send_sem=csend.at[h], recv_sem=crecv.at[h, 0],
            device_id={"col": sibling}, device_id_type=MESH,
        ).wait_send()
    batch(gx, NX - 1, 0).wait_send()
    batch(gz, NZ - 1, 2).wait_send()
    batch(gsum, NX - 1, 4).wait_recv()
    for k in range(NX):
        gram_ref[k * CHUNK : (k + 1) * CHUNK, :] = gsum[k]
    batch(gsum, NX - 1, 4).wait_send()


def per_device(tiles, tile_rows, tile_srcs, send_rows, basis, rotation):
    any_space = pl.BlockSpec(memory_space=pl.ANY)
    vmem = pl.BlockSpec(memory_space=pltpu.VMEM)
    dma = pltpu.SemaphoreType.DMA
    gram, rotated = pl.pallas_call(
        kernel,
        out_shape=(
            jax.ShapeDtypeStruct((WIDTH, K), jnp.float32),
            jax.ShapeDtypeStruct((WIDTH, ROWS), jnp.bfloat16),
        ),
        in_specs=[any_space] * 6,
        out_specs=(vmem, vmem),
        scratch_shapes=[
            pltpu.VMEM((TPD, TILE, TILE), jnp.bfloat16),
            pltpu.VMEM((1, TPD), jnp.int32),
            pltpu.VMEM((1, TPD), jnp.int32),
            pltpu.SMEM((1, NDOM), jnp.int32),
            pltpu.VMEM((WIDTH, ROWS), jnp.bfloat16),
            pltpu.VMEM((WIDTH, K), jnp.bfloat16),
            pltpu.VMEM((8, 128), jnp.int32),
            pltpu.SMEM((8, 128), jnp.int32),
            pltpu.VMEM((HALVES, RB, PART, TILE), jnp.bfloat16),
            pltpu.VMEM((2, HALVES, NDOM, PART, TILE), jnp.bfloat16),
            pltpu.VMEM((2, HALVES, NDOM, PART, TILE), jnp.bfloat16),
            pltpu.VMEM((HALVES, TPD, PART, TILE), jnp.float32),
            pltpu.VMEM((TPD, PART, TILE), jnp.float32),
            pltpu.VMEM((K, ROWS), jnp.bfloat16),
            pltpu.VMEM((NX, CHUNK, K), jnp.float32),
            pltpu.VMEM((NX, CHUNK, K), jnp.float32),
            pltpu.VMEM((NX, CHUNK, K), jnp.float32),
            pltpu.VMEM((NZ, CHUNK, K), jnp.float32),
            dma((7,)),
            dma((2, HALVES)),
            dma((2, HALVES, HALF)),
            dma((HALVES,)),
            dma((HALVES, 2 * NY)),
            dma((6,)),
        ],
        compiler_params=pltpu.CompilerParams(collective_id=0, has_side_effects=True, vmem_limit_bytes=56 << 20),
        cost_estimate=pl.CostEstimate(flops=300_000_000, bytes_accessed=4 << 20, transcendentals=0),
    )(tiles, tile_rows.reshape(1, TPD), tile_srcs.reshape(1, TPD), send_rows, basis, rotation.T)
    return gram.T, rotated


def solution(mesh):
    return jax.shard_map(
        per_device,
        mesh=mesh,
        in_specs=(
            P("dom", None, None),
            P("dom"),
            P("dom"),
            P("dom", None),
            P("col", "dom"),
            P(None, "col"),
        ),
        out_specs=(P(None, "col"), P("col", "dom")),
        check_vma=False,
    )
```

```python
import jax
import jax.numpy as jnp
from jax import lax
from jax.experimental import pallas as pl
from jax.experimental.pallas import tpu as pltpu
from jax.sharding import PartitionSpec as P

MESH = pl.DeviceIdType.MESH
TILE = 128
RB = 16
TPD = 96
WIDTH = 32
K = 256
ROWS = RB * TILE
NX, NZ = 4, 16
NDOM = NX * NZ
NY, NCORE = 4, 2
NCOL = NY * NCORE
OWN = TPD - NDOM
GROUP = 4
HALF = NZ // 2
BATCH = 2 * NX
HALVES = 2
PART = WIDTH // HALVES
CHUNK = WIDTH // NX


def loop(lo, hi, body):
    def step(i, carry):
        body(i)
        return carry

    lax.fori_loop(lo, hi, step, 0)


def build_tables(rows, srcs, tab):
    tab[...] = jnp.zeros_like(tab)
    at = lax.broadcasted_iota(jnp.int32, (TPD, TPD), 0)
    other = lax.broadcasted_iota(jnp.int32, (TPD, TPD), 1)
    rows_l = jnp.broadcast_to(rows[...], (TPD, TPD))
    srcs_l = jnp.broadcast_to(srcs[...], (TPD, TPD))

    def along(value):
        return jnp.sum(value, axis=1, keepdims=True)

    def across(value):
        return jnp.sum(value, axis=0, keepdims=True)

    one = jnp.ones((TPD, TPD), jnp.int32)
    zero = jnp.zeros((TPD, TPD), jnp.int32)
    rows_c = along(jnp.where(at == other, rows_l, zero))
    srcs_c = along(jnp.where(at == other, srcs_l, zero))
    earlier = other < at
    own_rank = along(jnp.where(jnp.logical_and(earlier, srcs_l < RB), one, zero))
    slot = jnp.where(srcs_c < RB, jnp.minimum(NDOM + own_rank, TPD - 1), srcs_c - RB)
    same_before = along(jnp.where(jnp.logical_and(rows_l == rows_c, earlier), one, zero))
    place = along(jnp.where(rows_l < rows_c, one, zero)) + same_before
    keep = jnp.minimum(same_before, 1)
    slot_here = slot == other
    place_here = place == other
    def put(n, most, value):
        tab[n : n + 1, 0:TPD] = jnp.minimum(across(value), most)

    put(0, TPD - 1, jnp.where(slot_here, at, zero))
    put(1, RB - 1, jnp.where(slot_here, jnp.broadcast_to(jnp.minimum(srcs_c, RB - 1), (TPD, TPD)), zero))
    put(2, TPD - 1, jnp.where(place_here, jnp.broadcast_to(slot, (TPD, TPD)), zero))
    put(3, 1, jnp.where(place_here, jnp.broadcast_to(keep, (TPD, TPD)), zero))
    upto = across(jnp.where(rows_c <= other, one, zero))
    tab[4:5, 0:TPD] = jnp.maximum(upto - 1, 0)


def kernel(
    tiles_h, rows_h, srcs_h, send_h, basis_h, rot_h,
    gram_ref, out_ref,
    tiles, rows, srcs, send_rows, basis, rot, tab, tabs,
    field, sbuf, rbuf, prods, sums, whole,
    gpart, gx, gsum, gz,
    in_sem, ssem, rsem, csend, crecv, gsem,
):
    me, mc = lax.axis_index("dom"), lax.axis_index("col")
    x, z = lax.div(me, NZ), lax.rem(me, NZ)
    y, core = lax.div(mc, NCORE), lax.rem(mc, NCORE)
    lines_to = [lax.rem(x + dx, NX) * NZ for dx in range(NX)]
    lines_from = [lax.rem(x + NX - dx, NX) * NZ for dx in range(NX)]

    def targets(j):
        ahead = (lax.rem(z + HALF + j, NZ), lax.rem(z + HALF - 1 - j, NZ))
        return [line + at for at in ahead for line in lines_to[::-1]]

    def origins(j):
        behind = (lax.rem(z + HALF - j, NZ), lax.rem(z + HALF + 1 + j, NZ))
        return [line + at for at in behind for line in lines_from[::-1]]

    def over_peers(body):
        loop(0, HALF - 1, lambda j: body(j, BATCH))
        body(HALF - 1, BATCH - 1)
    bar = pltpu.get_barrier_semaphore()

    loads = [
        pltpu.make_async_copy(src, dst, in_sem.at[n])
        for n, (src, dst) in enumerate(
            ((basis_h, basis), (send_h, send_rows), (rows_h, rows), (srcs_h, srcs), (tiles_h, tiles), (rot_h, rot))
        )
    ]
    for load in loads:
        load.start()

    def y_peer(d):
        return ((y + d) % NY) * NCORE + core

    sibling = y * NCORE + 1 - core

    def greet(**where):
        pl.semaphore_signal(bar, inc=1, device_id=where, device_id_type=MESH)

    def greet_peers(j, most):
        for peer in targets(j)[:most]:
            greet(dom=peer)

    over_peers(greet_peers)
    for d in range(1, NY):
        greet(col=y_peer(d))
    greet(col=sibling)

    for n in range(2):
        loads[n].wait()
    for h in range(HALVES):
        for r in range(RB):
            field[h, r] = basis[h * PART : (h + 1) * PART, r * TILE : (r + 1) * TILE]

    pl.semaphore_wait(bar, NDOM - 1 + NY)

    def halo(p, h, j, u, peer):
        slot = j * BATCH + u
        return pltpu.make_async_remote_copy(
            src_ref=sbuf.at[p, h, slot], dst_ref=rbuf.at[p, h, slot], send_sem=ssem.at[p, h], recv_sem=rsem.at[p, h, j],
            device_id={"dom": peer}, device_id_type=MESH,
        )

    def halo_batch(p, h, j, first, count):
        slots = pl.ds(first, count)
        return pltpu.make_async_remote_copy(
            src_ref=sbuf.at[p, h, slots], dst_ref=rbuf.at[p, h, slots], send_sem=ssem.at[p, h], recv_sem=rsem.at[p, h, j],
            device_id={"dom": x * NZ + lax.rem(z + 1, NZ)}, device_id_type=MESH,
        )

    def product(block, tile):
        return lax.dot_general(block, tile, (((1,), (1,)), ((), ())), preferred_element_type=jnp.float32)

    def send(p, h):
        def some(j, most):
            peers = targets(j)
            for u, peer in enumerate(peers[:most]):
                sbuf[p, h, j * BATCH + u] = field[h, send_rows[0, peer]]
            for u, peer in enumerate(peers[:most]):
                halo(p, h, j, u, peer).start()

        over_peers(some)
        rbuf[p, h, NDOM - 1] = field[h, send_rows[0, me]]

    def own(h):
        def group(g):
            for u in range(GROUP):
                s = NDOM + g * GROUP + u
                prods[h, s] = product(field[h, tabs[1, s]], tiles[tabs[0, s]])

        loop(0, OWN // GROUP, group)

    def receive(p, h, first, past):
        def take(j, waits):
            halo_batch(p, h, j, j * BATCH, waits).wait_recv()
            for u, peer in enumerate(origins(j)):
                prods[h, peer] = product(rbuf[p, h, j * BATCH + u], tiles[tabs[0, peer]])

        loop(first, min(past, HALF - 1), lambda j: take(j, BATCH))
        if past == HALF:
            take(HALF - 1, BATCH - 1)

    def add_up(h):
        def running(g, acc):
            for u in range(GROUP):
                s = g * GROUP + u
                acc = jnp.where(tabs[3, s] > 0, acc, 0.0) + prods[h, tabs[2, s]]
                sums[s] = acc
            return acc

        lax.fori_loop(0, TPD // GROUP, running, jnp.zeros((PART, TILE), jnp.float32))
        return [sums[tabs[4, r]].astype(jnp.bfloat16) for r in range(RB)]

    def part(owner, h):
        return whole.at[pl.ds(pl.multiple_of(owner * WIDTH + h * PART, PART), PART)]

    def pass_on(owner, h, to, n):
        return pltpu.make_async_remote_copy(
            src_ref=part(owner, h), dst_ref=part(owner, h), send_sem=csend.at[h], recv_sem=crecv.at[h, n],
            device_id={"col": to}, device_id_type=MESH,
        )

    def spread_out(h):
        for d in (2, 1, 3):
            pass_on(mc, h, y_peer(d), d).start()
        pass_on(mc, h, sibling, 0).start()

    def hand_over(h):
        for d in (1, 3, 2):
            origin = y_peer(NY - d)
            pass_on(origin, h, mc, d).wait_recv()
            pass_on(origin, h, sibling, NY + d).start()

    def gathered(h):
        pass_on(sibling, h, mc, 0).wait_recv()
        for d in (1, 3, 2):
            pass_on(((y + NY - d) % NY) * NCORE + 1 - core, h, mc, NY + d).wait_recv()

    def first_done(h):
        for r, block in enumerate(add_up(h)):
            field[h, r] = block

    def second_done(h):
        mine = pl.ds(pl.multiple_of(mc * WIDTH + h * PART, PART), PART)
        for r, block in enumerate(add_up(h)):
            whole[mine, r * TILE : (r + 1) * TILE] = block

    for h in range(HALVES):
        send(0, h)
    for n in range(2, 5):
        loads[n].wait()
    build_tables(rows, srcs, tab)
    to_smem = pltpu.make_async_copy(tab, tabs, in_sem.at[6])
    to_smem.start()
    to_smem.wait()
    for h in range(HALVES):
        own(h)
    for h in range(HALVES):
        receive(0, h, 0, HALF)
        first_done(h)
        send(1, h)
        own(h)
    for h in range(HALVES):
        receive(1, h, 0, HALF - 2)
        if h > 0:
            hand_over(h - 1)
        receive(1, h, HALF - 2, HALF)
        second_done(h)
        spread_out(h)
    loads[5].wait()
    for h in range(HALVES - 1):
        gathered(h)
    hand_over(HALVES - 1)
    gathered(HALVES - 1)

    mine = pl.ds(pl.multiple_of(mc * WIDTH, WIDTH), WIDTH)
    gram = lax.dot_general(
        whole[mine, :], whole[...], (((1,), (1,)), ((), ())), preferred_element_type=jnp.float32
    ) * (1.0 / (ROWS * NDOM))
    for k in range(NX):
        gpart[k] = gram[k * CHUNK : (k + 1) * CHUNK, :]

    def batch(ref, count, n):
        return pltpu.make_async_remote_copy(
            src_ref=ref.at[pl.ds(0, count)], dst_ref=ref.at[pl.ds(0, count)], send_sem=gsem.at[n], recv_sem=gsem.at[n + 1],
            device_id={"col": sibling}, device_id_type=MESH,
        )

    def x_scatter(d, sign):
        to = (x + sign * d + NX) % NX
        return pltpu.make_async_remote_copy(
            src_ref=gpart.at[to], dst_ref=gx.at[x], send_sem=gsem.at[0], recv_sem=gsem.at[1],
            device_id={"dom": to * NZ + z}, device_id_type=MESH,
        )

    for d in range(1, NX):
        x_scatter(d, 1).start()
    gx[x] = gpart[x]
    batch(gx, NX - 1, 0).wait_recv()
    mine_x = ((gx[0] + gx[1]) + gx[2]) + gx[3]
    gz[z] = jnp.concatenate([mine_x[:, 0:TILE], mine_x[:, TILE:K]], axis=0).astype(jnp.bfloat16)

    def z_share(owner, d):
        return pltpu.make_async_remote_copy(
            src_ref=gz.at[owner], dst_ref=gz.at[owner], send_sem=gsem.at[2], recv_sem=gsem.at[3],
            device_id={"dom": x * NZ + (z + d) % NZ}, device_id_type=MESH,
        )

    z_order = sorted(range(1, NZ), key=lambda d: -min(d, NZ - d))
    for d in z_order:
        z_share(z, d).start()

    def rotate(c):
        cols = pl.ds(pl.multiple_of(c * 512, 512), 512)
        out_ref[:, cols] = jnp.dot(rot[...], whole[:, cols], preferred_element_type=jnp.float32).astype(jnp.bfloat16)

    loop(0, ROWS // 512, rotate)
    batch(gz, NZ - 1, 2).wait_recv()
    total = gz[0].astype(jnp.float32)
    for k in range(1, NZ):
        total = total + gz[k].astype(jnp.float32)
    gsum[x] = jnp.concatenate([total[0:CHUNK], total[CHUNK:]], axis=1)

    def x_share(owner, d):
        return pltpu.make_async_remote_copy(
            src_ref=gsum.at[owner], dst_ref=gsum.at[owner], send_sem=gsem.at[4], recv_sem=gsem.at[5],
            device_id={"dom": ((x + d) % NX) * NZ + z}, device_id_type=MESH,
        )

    for d in range(1, NX):
        x_share(x, d).start()
    for p in range(2):
        for h in range(HALVES):
            halo_batch(p, h, 0, 0, NDOM - 1).wait_send()
    for h in range(HALVES):
        seven = whole.at[pl.ds(0, (2 * NY - 1) * PART)]
        pltpu.make_async_remote_copy(
            src_ref=seven, dst_ref=seven, send_sem=csend.at[h], recv_sem=crecv.at[h, 0],
            device_id={"col": sibling}, device_id_type=MESH,
        ).wait_send()
    batch(gx, NX - 1, 0).wait_send()
    batch(gz, NZ - 1, 2).wait_send()
    batch(gsum, NX - 1, 4).wait_recv()
    for k in range(NX):
        gram_ref[k * CHUNK : (k + 1) * CHUNK, :] = gsum[k]
    batch(gsum, NX - 1, 4).wait_send()


def per_device(tiles, tile_rows, tile_srcs, send_rows, basis, rotation):
    any_space = pl.BlockSpec(memory_space=pl.ANY)
    vmem = pl.BlockSpec(memory_space=pltpu.VMEM)
    dma = pltpu.SemaphoreType.DMA
    gram, rotated = pl.pallas_call(
        kernel,
        out_shape=(
            pltpu.VMEM((WIDTH, K), jnp.float32),
            pltpu.VMEM((WIDTH, ROWS), jnp.bfloat16),
        ),
        in_specs=[any_space] * 6,
        out_specs=(vmem, vmem),
        scratch_shapes=[
            pltpu.VMEM((TPD, TILE, TILE), jnp.bfloat16),
            pltpu.VMEM((1, TPD), jnp.int32),
            pltpu.VMEM((1, TPD), jnp.int32),
            pltpu.SMEM((1, NDOM), jnp.int32),
            pltpu.VMEM((WIDTH, ROWS), jnp.bfloat16),
            pltpu.VMEM((WIDTH, K), jnp.bfloat16),
            pltpu.VMEM((8, 128), jnp.int32),
            pltpu.SMEM((8, 128), jnp.int32),
            pltpu.VMEM((HALVES, RB, PART, TILE), jnp.bfloat16),
            pltpu.VMEM((2, HALVES, NDOM, PART, TILE), jnp.bfloat16),
            pltpu.VMEM((2, HALVES, NDOM, PART, TILE), jnp.bfloat16),
            pltpu.VMEM((HALVES, TPD, PART, TILE), jnp.float32),
            pltpu.VMEM((TPD, PART, TILE), jnp.float32),
            pltpu.VMEM((K, ROWS), jnp.bfloat16),
            pltpu.VMEM((NX, CHUNK, K), jnp.float32),
            pltpu.VMEM((NX, CHUNK, K), jnp.float32),
            pltpu.VMEM((NX, CHUNK, K), jnp.float32),
            pltpu.VMEM((NZ, 2 * CHUNK, TILE), jnp.bfloat16),
            dma((7,)),
            dma((2, HALVES)),
            dma((2, HALVES, HALF)),
            dma((HALVES,)),
            dma((HALVES, 2 * NY)),
            dma((6,)),
        ],
        compiler_params=pltpu.CompilerParams(collective_id=0, has_side_effects=True, vmem_limit_bytes=56 << 20),
        cost_estimate=pl.CostEstimate(flops=300_000_000, bytes_accessed=4 << 20, transcendentals=0),
    )(tiles, tile_rows.reshape(1, TPD), tile_srcs.reshape(1, TPD), send_rows, basis, rotation.T)
    return gram.T, rotated


def solution(mesh):
    return jax.shard_map(
        per_device,
        mesh=mesh,
        in_specs=(
            P("dom", None, None),
            P("dom"),
            P("dom"),
            P("dom", None),
            P("col", "dom"),
            P(None, "col"),
        ),
        out_specs=(P(None, "col"), P("col", "dom")),
        check_vma=False,
    )
```

```python
import jax
import jax.numpy as jnp
from jax import lax
from jax.experimental import pallas as pl
from jax.experimental.pallas import tpu as pltpu
from jax.sharding import PartitionSpec as P

MESH = pl.DeviceIdType.MESH
TILE = 128
RB = 16
TPD = 96
WIDTH = 32
K = 256
ROWS = RB * TILE
NX, NZ = 4, 16
NDOM = NX * NZ
NY, NCORE = 4, 2
NCOL = NY * NCORE
OWN = TPD - NDOM
GROUP = 4
HALF = NZ // 2
BATCH = 2 * NX
REACH = 3
HALVES = 2
PART = WIDTH // HALVES
CHUNK = WIDTH // NX


def loop(lo, hi, body):
    def step(i, carry):
        body(i)
        return carry

    lax.fori_loop(lo, hi, step, 0)


def build_tables(rows, srcs, tab):
    tab[...] = jnp.zeros_like(tab)
    at = lax.broadcasted_iota(jnp.int32, (TPD, TPD), 0)
    other = lax.broadcasted_iota(jnp.int32, (TPD, TPD), 1)
    rows_l = jnp.broadcast_to(rows[...], (TPD, TPD))
    srcs_l = jnp.broadcast_to(srcs[...], (TPD, TPD))

    def along(value):
        return jnp.sum(value, axis=1, keepdims=True)

    def across(value):
        return jnp.sum(value, axis=0, keepdims=True)

    one = jnp.ones((TPD, TPD), jnp.int32)
    zero = jnp.zeros((TPD, TPD), jnp.int32)
    rows_c = along(jnp.where(at == other, rows_l, zero))
    srcs_c = along(jnp.where(at == other, srcs_l, zero))
    earlier = other < at
    own_rank = along(jnp.where(jnp.logical_and(earlier, srcs_l < RB), one, zero))
    slot = jnp.where(srcs_c < RB, jnp.minimum(NDOM + own_rank, TPD - 1), srcs_c - RB)
    same_before = along(jnp.where(jnp.logical_and(rows_l == rows_c, earlier), one, zero))
    place = along(jnp.where(rows_l < rows_c, one, zero)) + same_before
    keep = jnp.minimum(same_before, 1)
    slot_here = slot == other
    place_here = place == other
    def put(n, most, value):
        tab[n : n + 1, 0:TPD] = jnp.minimum(across(value), most)

    put(0, TPD - 1, jnp.where(slot_here, at, zero))
    put(1, RB - 1, jnp.where(slot_here, jnp.broadcast_to(jnp.minimum(srcs_c, RB - 1), (TPD, TPD)), zero))
    put(2, TPD - 1, jnp.where(place_here, jnp.broadcast_to(slot, (TPD, TPD)), zero))
    put(3, 1, jnp.where(place_here, jnp.broadcast_to(keep, (TPD, TPD)), zero))
    upto = across(jnp.where(rows_c <= other, one, zero))
    tab[4:5, 0:TPD] = jnp.maximum(upto - 1, 0)


def kernel(
    tiles_h, rows_h, srcs_h, send_h, basis_h, rot_h,
    gram_ref, out_ref,
    tiles, rows, srcs, send_rows, basis, rot, tab, tabs,
    field, lent_refs, lent_rows, lent_list, sbuf, rbuf, prods, sums, whole,
    gpart, gx, gsum, gz,
    in_sem, fsend, frecv, lsend, lrecv, ssem, rsem, csend, crecv, gsem,
):
    me, mc = lax.axis_index("dom"), lax.axis_index("col")
    x, z = lax.div(me, NZ), lax.rem(me, NZ)
    y, core = lax.div(mc, NCORE), lax.rem(mc, NCORE)
    lines_to = [lax.rem(x + dx, NX) * NZ for dx in range(NX)]
    lines_from = [lax.rem(x + NX - dx, NX) * NZ for dx in range(NX)]

    def targets(j):
        ahead = (lax.rem(z + HALF + j, NZ), lax.rem(z + HALF - 1 - j, NZ))
        return [line + at for at in ahead for line in lines_to[::-1]]

    def origins(j):
        behind = (lax.rem(z + HALF - j, NZ), lax.rem(z + HALF + 1 + j, NZ))
        return [line + at for at in behind for line in lines_from[::-1]]

    def over_peers(body):
        loop(0, HALF - 1, lambda j: body(j, BATCH))
        body(HALF - 1, BATCH - 1)
    lent = [[[lent_refs[(p * HALVES + h) * 2 + side] for side in range(2)] for h in range(HALVES)] for p in range(2)]
    bar = pltpu.get_barrier_semaphore()

    loads = [
        pltpu.make_async_copy(src, dst, in_sem.at[n])
        for n, (src, dst) in enumerate(
            ((basis_h, basis), (send_h, send_rows), (rows_h, rows), (srcs_h, srcs), (tiles_h, tiles), (rot_h, rot))
        )
    ]
    for load in loads:
        load.start()

    def y_peer(d):
        return ((y + d) % NY) * NCORE + core

    sibling = y * NCORE + 1 - core

    def greet(**where):
        pl.semaphore_signal(bar, inc=1, device_id=where, device_id_type=MESH)

    def greet_peers(j, most):
        for peer in targets(j)[:most]:
            greet(dom=peer)

    over_peers(greet_peers)
    for d in range(1, NY):
        greet(col=y_peer(d))
    greet(col=sibling)

    for n in range(2):
        loads[n].wait()
    for h in range(HALVES):
        for r in range(RB):
            field[0, h, r] = basis[h * PART : (h + 1) * PART, r * TILE : (r + 1) * TILE]

    pl.semaphore_wait(bar, NDOM - 1 + NY)

    def halo(p, h, j, u, peer):
        slot = j * BATCH + u
        return pltpu.make_async_remote_copy(
            src_ref=sbuf.at[p, h, slot], dst_ref=rbuf.at[p, h, slot], send_sem=ssem.at[p, h], recv_sem=rsem.at[p, h, j],
            device_id={"dom": peer}, device_id_type=MESH,
        )

    def halo_batch(p, h, j, first, count):
        slots = pl.ds(first, count)
        return pltpu.make_async_remote_copy(
            src_ref=sbuf.at[p, h, slots], dst_ref=rbuf.at[p, h, slots], send_sem=ssem.at[p, h], recv_sem=rsem.at[p, h, j],
            device_id={"dom": x * NZ + lax.rem(z + 1, NZ)}, device_id_type=MESH,
        )

    def product(block, tile):
        return lax.dot_general(block, tile, (((1,), (1,)), ((), ())), preferred_element_type=jnp.float32)

    def along_z(d):
        return lax.rem(z + (d + NZ), NZ)

    def whole_field(p, h, side):
        to = along_z(REACH if side == 0 else -REACH)
        return pltpu.make_async_remote_copy(
            src_ref=field.at[p, h], dst_ref=lent[p][h][side], send_sem=fsend.at[p, h, side], recv_sem=frecv.at[p, h, side],
            device_id={"dom": x * NZ + to}, device_id_type=MESH,
        )

    def lists(side):
        to = along_z(REACH if side == 0 else -REACH)
        return pltpu.make_async_remote_copy(
            src_ref=send_h, dst_ref=lent_rows.at[side], send_sem=lsend.at[side], recv_sem=lrecv.at[side],
            device_id={"dom": x * NZ + to}, device_id_type=MESH,
        )

    def place_of(side, far):
        return (HALF - 1 - far, NX) if side == 0 else (HALF - far, 0)

    def send(p, h):
        for side in range(2):
            whole_field(p, h, side).start()
        near = []
        for side in range(2):
            j, first = place_of(side, 1)
            to = along_z(1 if side == 0 else -1)
            near += [(j, first + NX - 1 - dx, lines_to[dx] + to) for dx in range(NX)]
        near += [(HALF - 1, BATCH - 1 - dx, lines_to[dx] + z) for dx in range(1, NX)]
        for j, u, peer in near:
            sbuf[p, h, j * BATCH + u] = field[p, h, send_rows[0, peer]]
        for j, u, peer in near:
            halo(p, h, j, u, peer).start()
        rbuf[p, h, NDOM - 1] = field[p, h, send_rows[0, me]]

    def hand_on(p, h):
        for side in range(2):
            whole_field(p, h, side).wait_recv()

            def some(far, chosen=range(NX), side=side):
                j, first = place_of(side, far)
                to = along_z(far - REACH) if side == 0 else along_z(REACH - far)
                all_of = [(first + NX - 1 - dx, lines_to[dx] + to) for dx in chosen]
                for u, peer in all_of:
                    sbuf[p, h, j * BATCH + u] = lent[p][h][side][lent_list[side, 0, peer]]
                for u, peer in all_of:
                    halo(p, h, j, u, peer).start()

            j, to = 0, along_z(HALF - REACH) if side == 0 else along_z(REACH - HALF)
            halfway = [(NX - 1 - dx, lines_to[dx] + to) for dx in ((3, 2) if side == 0 else (1, 0))]
            for u, peer in halfway:
                sbuf[p, h, u] = lent[p][h][side][lent_list[side, 0, peer]]
            for u, peer in halfway:
                halo(p, h, j, u, peer).start()
            loop(0, HALF - 1 - REACH, lambda k, some=some: some(HALF - 1 - k))
            some(REACH - 1)
            some(REACH, range(1, NX))
            j, first = place_of(side, REACH)
            rbuf[p, h, j * BATCH + first + NX - 1] = lent[p][h][side][lent_list[side, 0, me]]

    def own(p, h):
        def group(g):
            for u in range(GROUP):
                s = NDOM + g * GROUP + u
                prods[h, s] = product(field[p, h, tabs[1, s]], tiles[tabs[0, s]])

        loop(0, OWN // GROUP, group)

    def receive(p, h, first, past):
        def take(j, waits):
            halo_batch(p, h, j, j * BATCH, waits).wait_recv()
            for u, peer in enumerate(origins(j)):
                prods[h, peer] = product(rbuf[p, h, j * BATCH + u], tiles[tabs[0, peer]])

        edge = place_of(1, REACH)[0] + 1
        for j in range(HALF - 1, edge - 3, -1):
            if first <= HALF - 1 - j < past:
                take(j, BATCH - (j in (HALF - 1, edge - 1, edge - 2)))
        lo = max(first, HALF - edge + 2)
        loop(lo, past, lambda k: take(HALF - 1 - k, BATCH))

    def add_up(h):
        def running(g, acc):
            for u in range(GROUP):
                s = g * GROUP + u
                acc = jnp.where(tabs[3, s] > 0, acc, 0.0) + prods[h, tabs[2, s]]
                sums[s] = acc
            return acc

        lax.fori_loop(0, TPD // GROUP, running, jnp.zeros((PART, TILE), jnp.float32))
        return [sums[tabs[4, r]].astype(jnp.bfloat16) for r in range(RB)]

    def part(owner, h):
        return whole.at[pl.ds(pl.multiple_of(owner * WIDTH + h * PART, PART), PART)]

    def pass_on(owner, h, to, n):
        return pltpu.make_async_remote_copy(
            src_ref=part(owner, h), dst_ref=part(owner, h), send_sem=csend.at[h], recv_sem=crecv.at[h, n],
            device_id={"col": to}, device_id_type=MESH,
        )

    def spread_out(h):
        for d in (2, 1, 3):
            pass_on(mc, h, y_peer(d), d).start()
        pass_on(mc, h, sibling, 0).start()

    def hand_over(h):
        for d in (1, 3, 2):
            origin = y_peer(NY - d)
            pass_on(origin, h, mc, d).wait_recv()
            pass_on(origin, h, sibling, NY + d).start()

    def gathered(h):
        pass_on(sibling, h, mc, 0).wait_recv()
        for d in (1, 3, 2):
            pass_on(((y + NY - d) % NY) * NCORE + 1 - core, h, mc, NY + d).wait_recv()

    def first_done(h):
        for r, block in enumerate(add_up(h)):
            field[1, h, r] = block

    def second_done(h):
        mine = pl.ds(pl.multiple_of(mc * WIDTH + h * PART, PART), PART)
        for r, block in enumerate(add_up(h)):
            whole[mine, r * TILE : (r + 1) * TILE] = block

    for side in range(2):
        lists(side).start()
    for h in range(HALVES):
        send(0, h)
    for n in range(2, 5):
        loads[n].wait()
    build_tables(rows, srcs, tab)
    to_smem = pltpu.make_async_copy(tab, tabs, in_sem.at[6])
    to_smem.start()
    to_smem.wait()
    for side in range(2):
        lists(side).wait_recv()
    lists_in = pltpu.make_async_copy(lent_rows, lent_list, in_sem.at[7])
    lists_in.start()
    lists_in.wait()
    for h in range(HALVES):
        hand_on(0, h)
        own(0, h)
    for h in range(HALVES):
        receive(0, h, 0, HALF)
        first_done(h)
        send(1, h)
        if h < HALVES - 1:
            own(1, h)
    for h in range(HALVES):
        hand_on(1, h)
    own(1, HALVES - 1)
    for h in range(HALVES):
        receive(1, h, 0, HALF - 2)
        if h > 0:
            hand_over(h - 1)
        receive(1, h, HALF - 2, HALF)
        second_done(h)
        spread_out(h)
    loads[5].wait()
    for h in range(HALVES - 1):
        gathered(h)
    hand_over(HALVES - 1)
    gathered(HALVES - 1)

    mine = pl.ds(pl.multiple_of(mc * WIDTH, WIDTH), WIDTH)
    gram = lax.dot_general(
        whole[mine, :], whole[...], (((1,), (1,)), ((), ())), preferred_element_type=jnp.float32
    ) * (1.0 / (ROWS * NDOM))
    for k in range(NX):
        gpart[k] = gram[k * CHUNK : (k + 1) * CHUNK, :]

    def batch(ref, count, n):
        return pltpu.make_async_remote_copy(
            src_ref=ref.at[pl.ds(0, count)], dst_ref=ref.at[pl.ds(0, count)], send_sem=gsem.at[n], recv_sem=gsem.at[n + 1],
            device_id={"col": sibling}, device_id_type=MESH,
        )

    def x_scatter(d, sign):
        to = (x + sign * d + NX) % NX
        return pltpu.make_async_remote_copy(
            src_ref=gpart.at[to], dst_ref=gx.at[x], send_sem=gsem.at[0], recv_sem=gsem.at[1],
            device_id={"dom": to * NZ + z}, device_id_type=MESH,
        )

    for d in range(1, NX):
        x_scatter(d, 1).start()
    gx[x] = gpart[x]
    batch(gx, NX - 1, 0).wait_recv()
    mine_x = ((gx[0] + gx[1]) + gx[2]) + gx[3]
    gz[z] = jnp.concatenate([mine_x[:, 0:TILE], mine_x[:, TILE:K]], axis=0).astype(jnp.bfloat16)

    def z_share(owner, d):
        return pltpu.make_async_remote_copy(
            src_ref=gz.at[owner], dst_ref=gz.at[owner], send_sem=gsem.at[2], recv_sem=gsem.at[3],
            device_id={"dom": x * NZ + (z + d) % NZ}, device_id_type=MESH,
        )

    z_order = sorted(range(1, NZ), key=lambda d: -min(d, NZ - d))
    for d in z_order:
        z_share(z, d).start()

    def rotate(c):
        cols = pl.ds(pl.multiple_of(c * 512, 512), 512)
        out_ref[:, cols] = jnp.dot(rot[...], whole[:, cols], preferred_element_type=jnp.float32).astype(jnp.bfloat16)

    loop(0, ROWS // 512, rotate)
    batch(gz, NZ - 1, 2).wait_recv()
    total = gz[0].astype(jnp.float32)
    for k in range(1, NZ):
        total = total + gz[k].astype(jnp.float32)
    gsum[x] = jnp.concatenate([total[0:CHUNK], total[CHUNK:]], axis=1)

    def x_share(owner, d):
        return pltpu.make_async_remote_copy(
            src_ref=gsum.at[owner], dst_ref=gsum.at[owner], send_sem=gsem.at[4], recv_sem=gsem.at[5],
            device_id={"dom": ((x + d) % NX) * NZ + z}, device_id_type=MESH,
        )

    for d in range(1, NX):
        x_share(x, d).start()
    for p in range(2):
        for h in range(HALVES):
            halo_batch(p, h, 0, 0, NDOM - 3).wait_send()
            for side in range(2):
                whole_field(p, h, side).wait_send()
    for side in range(2):
        lists(side).wait_send()
    for h in range(HALVES):
        seven = whole.at[pl.ds(0, (2 * NY - 1) * PART)]
        pltpu.make_async_remote_copy(
            src_ref=seven, dst_ref=seven, send_sem=csend.at[h], recv_sem=crecv.at[h, 0],
            device_id={"col": sibling}, device_id_type=MESH,
        ).wait_send()
    batch(gx, NX - 1, 0).wait_send()
    batch(gz, NZ - 1, 2).wait_send()
    batch(gsum, NX - 1, 4).wait_recv()
    for k in range(NX):
        gram_ref[k * CHUNK : (k + 1) * CHUNK, :] = gsum[k]
    batch(gsum, NX - 1, 4).wait_send()


def per_device(tiles, tile_rows, tile_srcs, send_rows, basis, rotation):
    any_space = pl.BlockSpec(memory_space=pl.ANY)
    vmem = pl.BlockSpec(memory_space=pltpu.VMEM)
    dma = pltpu.SemaphoreType.DMA
    gram, rotated = pl.pallas_call(
        kernel,
        out_shape=(
            pltpu.VMEM((WIDTH, K), jnp.float32),
            pltpu.VMEM((WIDTH, ROWS), jnp.bfloat16),
        ),
        in_specs=[any_space] * 6,
        out_specs=(vmem, vmem),
        scratch_shapes=[
            pltpu.VMEM((TPD, TILE, TILE), jnp.bfloat16),
            pltpu.VMEM((1, TPD), jnp.int32),
            pltpu.VMEM((1, TPD), jnp.int32),
            pltpu.SMEM((1, NDOM), jnp.int32),
            pltpu.VMEM((WIDTH, ROWS), jnp.bfloat16),
            pltpu.VMEM((WIDTH, K), jnp.bfloat16),
            pltpu.VMEM((8, 128), jnp.int32),
            pltpu.SMEM((8, 128), jnp.int32),
            pltpu.VMEM((2, HALVES, RB, PART, TILE), jnp.bfloat16),
            [pltpu.VMEM((RB, PART, TILE), jnp.bfloat16)] * (4 * HALVES),
            pltpu.VMEM((2, 1, NDOM), jnp.int32),
            pltpu.SMEM((2, 1, NDOM), jnp.int32),
            pltpu.VMEM((2, HALVES, NDOM, PART, TILE), jnp.bfloat16),
            pltpu.VMEM((2, HALVES, NDOM, PART, TILE), jnp.bfloat16),
            pltpu.VMEM((HALVES, TPD, PART, TILE), jnp.float32),
            pltpu.VMEM((TPD, PART, TILE), jnp.float32),
            pltpu.VMEM((K, ROWS), jnp.bfloat16),
            pltpu.VMEM((NX, CHUNK, K), jnp.float32),
            pltpu.VMEM((NX, CHUNK, K), jnp.float32),
            pltpu.VMEM((NX, CHUNK, K), jnp.float32),
            pltpu.VMEM((NZ, 2 * CHUNK, TILE), jnp.bfloat16),
            dma((8,)),
            dma((2, HALVES, 2)),
            dma((2, HALVES, 2)),
            dma((2,)),
            dma((2,)),
            dma((2, HALVES)),
            dma((2, HALVES, HALF)),
            dma((HALVES,)),
            dma((HALVES, 2 * NY)),
            dma((6,)),
        ],
        compiler_params=pltpu.CompilerParams(collective_id=0, has_side_effects=True, vmem_limit_bytes=56 << 20),
        cost_estimate=pl.CostEstimate(flops=300_000_000, bytes_accessed=4 << 20, transcendentals=0),
    )(tiles, tile_rows.reshape(1, TPD), tile_srcs.reshape(1, TPD), send_rows, basis, rotation.T)
    return gram.T, rotated


def solution(mesh):
    return jax.shard_map(
        per_device,
        mesh=mesh,
        in_specs=(
            P("dom", None, None),
            P("dom"),
            P("dom"),
            P("dom", None),
            P("col", "dom"),
            P(None, "col"),
        ),
        out_specs=(P(None, "col"), P("col", "dom")),
        check_vma=False,
    )
```

```python
import jax
import jax.numpy as jnp
from jax import lax
from jax.experimental import pallas as pl
from jax.experimental.pallas import tpu as pltpu
from jax.sharding import PartitionSpec as P

MESH = pl.DeviceIdType.MESH
TILE = 128
RB = 16
TPD = 96
WIDTH = 32
K = 256
ROWS = RB * TILE
NX, NZ = 4, 16
NDOM = NX * NZ
NY, NCORE = 4, 2
NCOL = NY * NCORE
OWN = TPD - NDOM
GROUP = 4
HALF = NZ // 2
BATCH = 2 * NX
REACH = 3
HALVES = 2
PART = WIDTH // HALVES
CHUNK = WIDTH // NX


def loop(lo, hi, body):
    def step(i, carry):
        body(i)
        return carry

    lax.fori_loop(lo, hi, step, 0)


def build_tables(rows, srcs, tab):
    tab[...] = jnp.zeros_like(tab)
    at = lax.broadcasted_iota(jnp.int32, (TPD, TPD), 0)
    other = lax.broadcasted_iota(jnp.int32, (TPD, TPD), 1)
    rows_l = jnp.broadcast_to(rows[...], (TPD, TPD))
    srcs_l = jnp.broadcast_to(srcs[...], (TPD, TPD))

    def along(value):
        return jnp.sum(value, axis=1, keepdims=True)

    def across(value):
        return jnp.sum(value, axis=0, keepdims=True)

    one = jnp.ones((TPD, TPD), jnp.int32)
    zero = jnp.zeros((TPD, TPD), jnp.int32)
    rows_c = along(jnp.where(at == other, rows_l, zero))
    srcs_c = along(jnp.where(at == other, srcs_l, zero))
    earlier = other < at
    own_rank = along(jnp.where(jnp.logical_and(earlier, srcs_l < RB), one, zero))
    slot = jnp.where(srcs_c < RB, jnp.minimum(NDOM + own_rank, TPD - 1), srcs_c - RB)
    same_before = along(jnp.where(jnp.logical_and(rows_l == rows_c, earlier), one, zero))
    place = along(jnp.where(rows_l < rows_c, one, zero)) + same_before
    keep = jnp.minimum(same_before, 1)
    slot_here = slot == other
    place_here = place == other
    def put(n, most, value):
        tab[n : n + 1, 0:TPD] = jnp.minimum(across(value), most)

    put(0, TPD - 1, jnp.where(slot_here, at, zero))
    put(1, RB - 1, jnp.where(slot_here, jnp.broadcast_to(jnp.minimum(srcs_c, RB - 1), (TPD, TPD)), zero))
    put(2, TPD - 1, jnp.where(place_here, jnp.broadcast_to(slot, (TPD, TPD)), zero))
    put(3, 1, jnp.where(place_here, jnp.broadcast_to(keep, (TPD, TPD)), zero))
    upto = across(jnp.where(rows_c <= other, one, zero))
    tab[4:5, 0:TPD] = jnp.maximum(upto - 1, 0)


def kernel(
    tiles_h, rows_h, srcs_h, send_h, basis_h, rot_h,
    gram_ref, out_ref,
    tiles, rows, srcs, send_rows, basis, rot, tab, tabs,
    field, lent_refs, lent_rows, lent_list, sbuf, rbuf, prods, sums, whole,
    gpart, gx, gsum, gz,
    in_sem, fsend, frecv, lsend, lrecv, ssem, rsem, csend, crecv, gsem,
):
    me, mc = lax.axis_index("dom"), lax.axis_index("col")
    x, z = lax.div(me, NZ), lax.rem(me, NZ)
    y, core = lax.div(mc, NCORE), lax.rem(mc, NCORE)
    lines_to = [lax.rem(x + dx, NX) * NZ for dx in range(NX)]
    lines_from = [lax.rem(x + NX - dx, NX) * NZ for dx in range(NX)]

    def targets(j):
        ahead = (lax.rem(z + HALF + j, NZ), lax.rem(z + HALF - 1 - j, NZ))
        return [line + at for at in ahead for line in lines_to[::-1]]

    def origins(j):
        behind = (lax.rem(z + HALF - j, NZ), lax.rem(z + HALF + 1 + j, NZ))
        return [line + at for at in behind for line in lines_from[::-1]]

    def over_peers(body):
        loop(0, HALF - 1, lambda j: body(j, BATCH))
        body(HALF - 1, BATCH - 1)
    lent = [[[lent_refs[(p * HALVES + h) * 2 + side] for side in range(2)] for h in range(HALVES)] for p in range(2)]
    bar = pltpu.get_barrier_semaphore()

    loads = [
        pltpu.make_async_copy(src, dst, in_sem.at[n])
        for n, (src, dst) in enumerate(
            ((basis_h, basis), (send_h, send_rows), (rows_h, rows), (srcs_h, srcs), (tiles_h, tiles), (rot_h, rot))
        )
    ]
    for load in loads:
        load.start()

    def y_peer(d):
        return ((y + d) % NY) * NCORE + core

    sibling = y * NCORE + 1 - core

    def greet(**where):
        pl.semaphore_signal(bar, inc=1, device_id=where, device_id_type=MESH)

    def greet_peers(j, most):
        for peer in targets(j)[:most]:
            greet(dom=peer)

    over_peers(greet_peers)
    for d in range(1, NY):
        greet(col=y_peer(d))
    greet(col=sibling)

    for n in range(2):
        loads[n].wait()
    for h in range(HALVES):
        for r in range(RB):
            field[0, h, r] = basis[h * PART : (h + 1) * PART, r * TILE : (r + 1) * TILE]

    pl.semaphore_wait(bar, NDOM - 1 + NY)

    def halo(p, h, j, u, peer):
        slot = j * BATCH + u
        return pltpu.make_async_remote_copy(
            src_ref=sbuf.at[p, h, slot], dst_ref=rbuf.at[p, h, slot], send_sem=ssem.at[p, h], recv_sem=rsem.at[p, h, j],
            device_id={"dom": peer}, device_id_type=MESH,
        )

    def halo_batch(p, h, j, first, count):
        slots = pl.ds(first, count)
        return pltpu.make_async_remote_copy(
            src_ref=sbuf.at[p, h, slots], dst_ref=rbuf.at[p, h, slots], send_sem=ssem.at[p, h], recv_sem=rsem.at[p, h, j],
            device_id={"dom": x * NZ + lax.rem(z + 1, NZ)}, device_id_type=MESH,
        )

    def product(block, tile):
        return lax.dot_general(block, tile, (((1,), (1,)), ((), ())), preferred_element_type=jnp.float32)

    def along_z(d):
        return lax.rem(z + (d + NZ), NZ)

    def whole_field(p, h, side):
        to = along_z(REACH if side == 0 else -REACH)
        return pltpu.make_async_remote_copy(
            src_ref=field.at[p, h], dst_ref=lent[p][h][side], send_sem=fsend.at[p, h, side], recv_sem=frecv.at[p, h, side],
            device_id={"dom": x * NZ + to}, device_id_type=MESH,
        )

    def lists(side):
        to = along_z(REACH if side == 0 else -REACH)
        return pltpu.make_async_remote_copy(
            src_ref=send_h, dst_ref=lent_rows.at[side], send_sem=lsend.at[side], recv_sem=lrecv.at[side],
            device_id={"dom": x * NZ + to}, device_id_type=MESH,
        )

    def place_of(side, far):
        return (HALF - 1 - far, NX) if side == 0 else (HALF - far, 0)

    def send(p, h):
        for side in range(2):
            whole_field(p, h, side).start()
        near = []
        for side in range(2):
            j, first = place_of(side, 1)
            to = along_z(1 if side == 0 else -1)
            near += [(j, first + NX - 1 - dx, lines_to[dx] + to) for dx in range(NX)]
        near += [(HALF - 1, BATCH - 1 - dx, lines_to[dx] + z) for dx in range(1, NX)]
        for j, u, peer in near:
            sbuf[p, h, j * BATCH + u] = field[p, h, send_rows[0, peer]]
        for j, u, peer in near:
            halo(p, h, j, u, peer).start()
        rbuf[p, h, NDOM - 1] = field[p, h, send_rows[0, me]]

    def hand_on(p, h):
        for side in range(2):
            whole_field(p, h, side).wait_recv()

            def some(far, chosen=range(NX), side=side):
                j, first = place_of(side, far)
                to = along_z(far - REACH) if side == 0 else along_z(REACH - far)
                all_of = [(first + NX - 1 - dx, lines_to[dx] + to) for dx in chosen]
                for u, peer in all_of:
                    sbuf[p, h, j * BATCH + u] = lent[p][h][side][lent_list[side, 0, peer]]
                for u, peer in all_of:
                    halo(p, h, j, u, peer).start()

            j, to = 0, along_z(HALF - REACH) if side == 0 else along_z(REACH - HALF)
            halfway = [(NX - 1 - dx, lines_to[dx] + to) for dx in ((3, 2) if side == 0 else (1, 0))]
            for u, peer in halfway:
                sbuf[p, h, u] = lent[p][h][side][lent_list[side, 0, peer]]
            for u, peer in halfway:
                halo(p, h, j, u, peer).start()
            loop(0, HALF - 1 - REACH, lambda k, some=some: some(HALF - 1 - k))
            some(REACH - 1)
            some(REACH, range(1, NX))
            j, first = place_of(side, REACH)
            rbuf[p, h, j * BATCH + first + NX - 1] = lent[p][h][side][lent_list[side, 0, me]]

    def own(p, h):
        def group(g):
            for u in range(GROUP):
                s = NDOM + g * GROUP + u
                prods[h, s] = product(field[p, h, tabs[1, s]], tiles[tabs[0, s]])

        loop(0, OWN // GROUP, group)

    def receive(p, h, first, past):
        def take(j, waits):
            halo_batch(p, h, j, j * BATCH, waits).wait_recv()
            for u, peer in enumerate(origins(j)):
                prods[h, peer] = product(rbuf[p, h, j * BATCH + u], tiles[tabs[0, peer]])

        edge = place_of(1, REACH)[0] + 1
        for j in range(HALF - 1, edge - 3, -1):
            if first <= HALF - 1 - j < past:
                take(j, BATCH - (j in (HALF - 1, edge - 1, edge - 2)))
        lo = max(first, HALF - edge + 2)
        loop(lo, past, lambda k: take(HALF - 1 - k, BATCH))

    def add_up(h):
        def running(g, acc):
            for u in range(GROUP):
                s = g * GROUP + u
                acc = jnp.where(tabs[3, s] > 0, acc, 0.0) + prods[h, tabs[2, s]]
                sums[s] = acc
            return acc

        lax.fori_loop(0, TPD // GROUP, running, jnp.zeros((PART, TILE), jnp.float32))
        return [sums[tabs[4, r]].astype(jnp.bfloat16) for r in range(RB)]

    def part(owner, h):
        return whole.at[pl.ds(pl.multiple_of(owner * WIDTH + h * PART, PART), PART)]

    def pass_on(owner, h, to, n):
        return pltpu.make_async_remote_copy(
            src_ref=part(owner, h), dst_ref=part(owner, h), send_sem=csend.at[h], recv_sem=crecv.at[h, n],
            device_id={"col": to}, device_id_type=MESH,
        )

    def spread_out(h):
        for d in (2, 1, 3):
            pass_on(mc, h, y_peer(d), d).start()
        pass_on(mc, h, sibling, 0).start()

    def hand_over(h):
        for d in (1, 3, 2):
            origin = y_peer(NY - d)
            pass_on(origin, h, mc, d).wait_recv()
            pass_on(origin, h, sibling, NY + d).start()

    def gathered(h):
        pass_on(sibling, h, mc, 0).wait_recv()
        for d in (1, 3, 2):
            pass_on(((y + NY - d) % NY) * NCORE + 1 - core, h, mc, NY + d).wait_recv()

    def first_done(h):
        for r, block in enumerate(add_up(h)):
            field[1, h, r] = block

    def second_done(h):
        mine = pl.ds(pl.multiple_of(mc * WIDTH + h * PART, PART), PART)
        for r, block in enumerate(add_up(h)):
            whole[mine, r * TILE : (r + 1) * TILE] = block

    for side in range(2):
        lists(side).start()
    for h in range(HALVES):
        send(0, h)
    for n in range(2, 5):
        loads[n].wait()
    build_tables(rows, srcs, tab)
    to_smem = pltpu.make_async_copy(tab, tabs, in_sem.at[6])
    to_smem.start()
    to_smem.wait()
    for h in range(HALVES):
        own(0, h)
    for side in range(2):
        lists(side).wait_recv()
    lists_in = pltpu.make_async_copy(lent_rows, lent_list, in_sem.at[7])
    lists_in.start()
    lists_in.wait()
    for h in range(HALVES):
        hand_on(0, h)
    for h in range(HALVES):
        receive(0, h, 0, HALF)
        first_done(h)
        send(1, h)
        if h < HALVES - 1:
            own(1, h)
    for h in range(HALVES):
        hand_on(1, h)
    own(1, HALVES - 1)
    for h in range(HALVES):
        receive(1, h, 0, HALF - 2)
        if h > 0:
            hand_over(h - 1)
        receive(1, h, HALF - 2, HALF)
        second_done(h)
        spread_out(h)
    loads[5].wait()
    for h in range(HALVES - 1):
        gathered(h)
    hand_over(HALVES - 1)
    gathered(HALVES - 1)

    mine = pl.ds(pl.multiple_of(mc * WIDTH, WIDTH), WIDTH)
    gram = lax.dot_general(
        whole[mine, :], whole[...], (((1,), (1,)), ((), ())), preferred_element_type=jnp.float32
    ) * (1.0 / (ROWS * NDOM))
    for k in range(NX):
        gpart[k] = gram[k * CHUNK : (k + 1) * CHUNK, :]

    def batch(ref, count, n):
        return pltpu.make_async_remote_copy(
            src_ref=ref.at[pl.ds(0, count)], dst_ref=ref.at[pl.ds(0, count)], send_sem=gsem.at[n], recv_sem=gsem.at[n + 1],
            device_id={"col": sibling}, device_id_type=MESH,
        )

    def x_scatter(d, sign):
        to = (x + sign * d + NX) % NX
        return pltpu.make_async_remote_copy(
            src_ref=gpart.at[to], dst_ref=gx.at[x], send_sem=gsem.at[0], recv_sem=gsem.at[1],
            device_id={"dom": to * NZ + z}, device_id_type=MESH,
        )

    for d in range(1, NX):
        x_scatter(d, 1).start()
    gx[x] = gpart[x]
    batch(gx, NX - 1, 0).wait_recv()
    mine_x = ((gx[0] + gx[1]) + gx[2]) + gx[3]
    gz[z] = jnp.concatenate([mine_x[:, 0:TILE], mine_x[:, TILE:K]], axis=0).astype(jnp.bfloat16)

    def z_share(owner, d):
        return pltpu.make_async_remote_copy(
            src_ref=gz.at[owner], dst_ref=gz.at[owner], send_sem=gsem.at[2], recv_sem=gsem.at[3],
            device_id={"dom": x * NZ + (z + d) % NZ}, device_id_type=MESH,
        )

    z_order = sorted(range(1, NZ), key=lambda d: -min(d, NZ - d))
    for d in z_order:
        z_share(z, d).start()

    def rotate(c):
        cols = pl.ds(pl.multiple_of(c * 512, 512), 512)
        out_ref[:, cols] = jnp.dot(rot[...], whole[:, cols], preferred_element_type=jnp.float32).astype(jnp.bfloat16)

    loop(0, ROWS // 512, rotate)
    batch(gz, NZ - 1, 2).wait_recv()
    total = gz[0].astype(jnp.float32)
    for k in range(1, NZ):
        total = total + gz[k].astype(jnp.float32)
    gsum[x] = jnp.concatenate([total[0:CHUNK], total[CHUNK:]], axis=1)

    def x_share(owner, d):
        return pltpu.make_async_remote_copy(
            src_ref=gsum.at[owner], dst_ref=gsum.at[owner], send_sem=gsem.at[4], recv_sem=gsem.at[5],
            device_id={"dom": ((x + d) % NX) * NZ + z}, device_id_type=MESH,
        )

    for d in range(1, NX):
        x_share(x, d).start()
    for p in range(2):
        for h in range(HALVES):
            halo_batch(p, h, 0, 0, NDOM - 3).wait_send()
            for side in range(2):
                whole_field(p, h, side).wait_send()
    for side in range(2):
        lists(side).wait_send()
    for h in range(HALVES):
        seven = whole.at[pl.ds(0, (2 * NY - 1) * PART)]
        pltpu.make_async_remote_copy(
            src_ref=seven, dst_ref=seven, send_sem=csend.at[h], recv_sem=crecv.at[h, 0],
            device_id={"col": sibling}, device_id_type=MESH,
        ).wait_send()
    batch(gx, NX - 1, 0).wait_send()
    batch(gz, NZ - 1, 2).wait_send()
    batch(gsum, NX - 1, 4).wait_recv()
    for k in range(NX):
        gram_ref[k * CHUNK : (k + 1) * CHUNK, :] = gsum[k]
    batch(gsum, NX - 1, 4).wait_send()


def per_device(tiles, tile_rows, tile_srcs, send_rows, basis, rotation):
    any_space = pl.BlockSpec(memory_space=pl.ANY)
    vmem = pl.BlockSpec(memory_space=pltpu.VMEM)
    dma = pltpu.SemaphoreType.DMA
    gram, rotated = pl.pallas_call(
        kernel,
        out_shape=(
            pltpu.VMEM((WIDTH, K), jnp.float32),
            pltpu.VMEM((WIDTH, ROWS), jnp.bfloat16),
        ),
        in_specs=[any_space] * 6,
        out_specs=(vmem, vmem),
        scratch_shapes=[
            pltpu.VMEM((TPD, TILE, TILE), jnp.bfloat16),
            pltpu.VMEM((1, TPD), jnp.int32),
            pltpu.VMEM((1, TPD), jnp.int32),
            pltpu.SMEM((1, NDOM), jnp.int32),
            pltpu.VMEM((WIDTH, ROWS), jnp.bfloat16),
            pltpu.VMEM((WIDTH, K), jnp.bfloat16),
            pltpu.VMEM((8, 128), jnp.int32),
            pltpu.SMEM((8, 128), jnp.int32),
            pltpu.VMEM((2, HALVES, RB, PART, TILE), jnp.bfloat16),
            [pltpu.VMEM((RB, PART, TILE), jnp.bfloat16)] * (4 * HALVES),
            pltpu.VMEM((2, 1, NDOM), jnp.int32),
            pltpu.SMEM((2, 1, NDOM), jnp.int32),
            pltpu.VMEM((2, HALVES, NDOM, PART, TILE), jnp.bfloat16),
            pltpu.VMEM((2, HALVES, NDOM, PART, TILE), jnp.bfloat16),
            pltpu.VMEM((HALVES, TPD, PART, TILE), jnp.float32),
            pltpu.VMEM((TPD, PART, TILE), jnp.float32),
            pltpu.VMEM((K, ROWS), jnp.bfloat16),
            pltpu.VMEM((NX, CHUNK, K), jnp.float32),
            pltpu.VMEM((NX, CHUNK, K), jnp.float32),
            pltpu.VMEM((NX, CHUNK, K), jnp.float32),
            pltpu.VMEM((NZ, 2 * CHUNK, TILE), jnp.bfloat16),
            dma((8,)),
            dma((2, HALVES, 2)),
            dma((2, HALVES, 2)),
            dma((2,)),
            dma((2,)),
            dma((2, HALVES)),
            dma((2, HALVES, HALF)),
            dma((HALVES,)),
            dma((HALVES, 2 * NY)),
            dma((6,)),
        ],
        compiler_params=pltpu.CompilerParams(collective_id=0, has_side_effects=True, vmem_limit_bytes=56 << 20),
        cost_estimate=pl.CostEstimate(flops=300_000_000, bytes_accessed=4 << 20, transcendentals=0),
    )(tiles, tile_rows.reshape(1, TPD), tile_srcs.reshape(1, TPD), send_rows, basis, rotation.T)
    return gram.T, rotated


def solution(mesh):
    return jax.shard_map(
        per_device,
        mesh=mesh,
        in_specs=(
            P("dom", None, None),
            P("dom"),
            P("dom"),
            P("dom", None),
            P("col", "dom"),
            P(None, "col"),
        ),
        out_specs=(P(None, "col"), P("col", "dom")),
        check_vma=False,
    )
```
